128 devices in a mesh: row: 16 (over y, x_lo, core), col: 8 (over x_hi, z).
Axes of the slice: x: 4 (x_hi: 2, x_lo: 2; x = x_hi * 2 + x_lo), y: 4, z: 4, core: 2. Of those that a mesh axis runs over, the one named last changes fastest.
Arguments:
- tokens: bfloat16 [256, 2048, 256], P('row', 'col'), may hold values from -6 to 6
- bn_scale: float32 [256], replicated, may hold values from 0.5 to 1.5
- bn_shift: float32 [256], replicated, may hold values from -3 to 3
- w_expand: bfloat16 [256, 1024], replicated, may hold values from -0.375 to 0.375
- b_expand: float32 [1024], replicated, may hold values from -3 to 3
- dw_kernel: float32 [3, 3, 1024], replicated, may hold values from -2 to 2
- dw_bias: float32 [1024], replicated, may hold values from -3 to 3
- w_project: bfloat16 [1024, 256], replicated, may hold values from -0.1875 to 0.1875
- b_project: float32 [256], replicated, may hold values from -3 to 3
- norm_gains: float32 [4, 256], replicated, may hold values from 0.5 to 1.5
- attn_qkv: bfloat16 [2, 256, 768], replicated, may hold values from -0.375 to 0.375
- attn_out: bfloat16 [2, 256, 256], replicated, may hold values from -0.375 to 0.375
- rel_bias: float32 [2, 8, 225], replicated, may hold values from -5 to 762
- mlp_up: bfloat16 [2, 256, 1024], replicated, may hold values from -0.375 to 0.375
- mlp_down: bfloat16 [2, 1024, 256], replicated, may hold values from -0.1875 to 0.1875
Outputs:
- block_out: bfloat16 [256, 2048, 256], P('row', 'col')
The draws below stay inside these ranges and needn't reach their ends.
All inputs are finite; a program needn't handle non-finite values.
Results may differ from the reference program's by a relative error of at most 0.018.
Values may be sent and summed in bfloat16 or wider, within the bound.
A program may use at most 128 MiB of HBM per device.

```python
import math
import jax
import jax.numpy as jnp
from jax import lax

C = 256
HID = 1024
HEADS = 8
WIN = 8
GRID = 8
IMG_R = 256
IMG_C = 2048


def draw_rel_bias(key, part):
    key = jax.random.fold_in(key, 7)
    n_entries = (2 * WIN - 1) * (2 * WIN - 1)
    return jnp.clip(jax.random.normal(key, (2, HEADS, n_entries), jnp.float32), -5.0, 5.0)


def block_levels(own_key, shape, cuts, smallest, high):
    level = 1.0
    for dim, parts in cuts:
        steps = jax.random.uniform(jax.random.fold_in(jax.random.fold_in(own_key, 6), dim), (parts,), jnp.float32, smallest / len(cuts), high / len(cuts))
        level = level * jnp.repeat(jnp.exp(steps), shape[dim] // parts).reshape((-1,) + (1,) * (len(shape) - 1 - dim))
    return level


def normal_values(stream_key, shape, scale, limit, shards=(), held_as=jnp.bfloat16):
    entries = jax.random.normal(stream_key, shape, jnp.float32) * scale
    if len(shards) > 0:
        entries = block_levels(stream_key, shape, shards, -0.22, 0.18) * entries
    return jnp.clip(entries, min=-limit, max=limit).astype(held_as)


def setup_inputs(seed: int = 0) -> dict:
    key_list = jax.random.split(jax.random.key(seed), 16)
    return {
        "tokens": normal_values(key_list[0], (IMG_R, IMG_C, C), 1.0, 6.0, ((0, 16), (1, 8))),
        "bn_scale": jnp.clip(jax.random.uniform(key_list[1], (C,), jnp.float32, 0.5, 1.5), 0.5, 1.5),
        "bn_shift": normal_values(key_list[2], (C,), 0.5, 3.0, (), jnp.float32),
        "w_expand": normal_values(key_list[3], (C, HID), C ** -0.5, 0.375),
        "b_expand": normal_values(key_list[4], (HID,), 0.5, 3.0, (), jnp.float32),
        "dw_kernel": normal_values(key_list[5], (3, 3, HID), 9 ** -0.5, 2.0, (), jnp.float32),
        "dw_bias": normal_values(key_list[6], (HID,), 0.5, 3.0, (), jnp.float32),
        "w_project": normal_values(key_list[7], (HID, C), HID ** -0.5, 0.1875),
        "b_project": normal_values(key_list[8], (C,), 0.5, 3.0, (), jnp.float32),
        "norm_gains": jnp.clip(jax.random.uniform(key_list[9], (4, C), jnp.float32, 0.5, 1.5), 0.5, 1.5),
        "attn_qkv": normal_values(key_list[10], (2, C, 3 * C), C ** -0.5, 0.375),
        "attn_out": normal_values(key_list[11], (2, C, C), C ** -0.5, 0.375),
        "rel_bias": draw_rel_bias(jax.random.fold_in(key_list[15], 71), 0),
        "mlp_up": normal_values(key_list[13], (2, C, HID), C ** -0.5, 0.375),
        "mlp_down": normal_values(key_list[14], (2, HID, C), HID ** -0.5, 0.1875),
    }


def table_index(window):
    places = jnp.arange(window * window, dtype=jnp.int32)
    across = places // window
    within = places % window
    row_part = (across[:, None] - across[None, :] + window - 1) * (2 * window - 1)
    return row_part + (within[:, None] - within[None, :] + window - 1)

def layer_norm(values, gain):
    center = values - lax.optimization_barrier(jnp.mean(values, axis=-1, keepdims=True))
    spread = lax.optimization_barrier(jnp.mean(center * center, axis=-1, keepdims=True))
    return center * lax.rsqrt(spread + 1e-05) * gain

def attend(windows, gain, w_qkv, w_out, bias_full):
    n_windows, per_window, features = windows.shape
    n_heads = bias_full.shape[0]
    head_size = features // n_heads
    values = windows.astype(jnp.float32)
    normed = layer_norm(values, gain).astype(jnp.bfloat16)
    packed = jnp.dot(normed.reshape(-1, features), w_qkv, preferred_element_type=jnp.float32).astype(jnp.bfloat16)
    packed = packed.reshape(n_windows, per_window, 3, n_heads, head_size).astype(jnp.float32)
    queries = packed[:, :, 0]
    key_part = packed[:, :, 1]
    value_part = packed[:, :, 2]
    scores = jnp.einsum('nqhd,nkhd->nhqk', queries, key_part) * head_size ** (-0.5) + bias_full[None]
    weights = jax.nn.softmax(scores, axis=-1).astype(jnp.bfloat16)
    context = jnp.einsum('nhqk,nkhd->nqhd', weights.astype(jnp.float32), value_part).astype(jnp.bfloat16)
    context = context.reshape(-1, features)
    result = values.reshape(-1, features) + jnp.dot(context, w_out, preferred_element_type=jnp.float32)
    return result.astype(jnp.bfloat16).reshape(n_windows, per_window, features)

def attend_all(windows, gain, w_qkv, w_out, bias_full):
    n_windows, per_window, features = windows.shape
    per_block = math.gcd(n_windows, 128)
    grouped = windows.reshape(n_windows // per_block, per_block, per_window, features)
    result = lax.map(lambda group: attend(group, gain, w_qkv, w_out, bias_full), grouped)
    return result.reshape(n_windows, per_window, features)

def feed_forward(flat, gain, w_up, w_down):
    values = flat.astype(jnp.float32)
    normed = layer_norm(values, gain).astype(jnp.bfloat16)
    inner_act = jax.nn.gelu(jnp.dot(normed, w_up, preferred_element_type=jnp.float32)).astype(jnp.bfloat16)
    return (values + jnp.dot(inner_act, w_down, preferred_element_type=jnp.float32)).astype(jnp.bfloat16)

def mlp_all(flat, gain, w_up, w_down):
    n_tokens, features = flat.shape
    per_block = math.gcd(n_tokens, 8192)
    grouped = flat.reshape(n_tokens // per_block, per_block, features)
    result = lax.map(lambda group: feed_forward(group, gain, w_up, w_down), grouped)
    return result.reshape(n_tokens, features)

def mbconv(tokens, bn_scale, bn_shift, w_expand, b_expand, dw_kernel, dw_bias, w_project, b_project):
    height, breadth, features = tokens.shape
    band_rows = math.gcd(height, 32)
    n_bands = height // band_rows
    padded_in = jnp.pad(tokens, ((1, 1), (0, 0), (0, 0)))

    def one_band(band_idx):
        band_start = (band_idx * band_rows).astype(jnp.int32)
        slab_rows = lax.dynamic_slice_in_dim(padded_in, band_start, band_rows + 2, 0)
        normed = (slab_rows.astype(jnp.float32) * bn_scale + bn_shift).astype(jnp.bfloat16)
        inner_act = jnp.dot(normed.reshape(-1, features), w_expand, preferred_element_type=jnp.float32) + b_expand
        hidden = jax.nn.gelu(inner_act).astype(jnp.bfloat16).reshape(band_rows + 2, breadth, -1)
        row_pos = band_start + jnp.arange(band_rows + 2, dtype=jnp.int32) - 1
        keep_rows = ((row_pos >= 0) & (row_pos < height)).astype(jnp.bfloat16)
        hidden = hidden * keep_rows[:, None, None]
        hidden = jnp.pad(hidden, ((0, 0), (1, 1), (0, 0)))
        summed = jnp.zeros((band_rows, breadth, hidden.shape[2]), jnp.float32) + dw_bias
        for off_r in range(3):
            for off_c in range(3):
                summed = summed + hidden[off_r:off_r + band_rows, off_c:off_c + breadth].astype(jnp.float32) * dw_kernel[off_r, off_c]
        activated = jax.nn.gelu(summed).astype(jnp.bfloat16).reshape(band_rows * breadth, -1)
        own_rows = slab_rows[1:-1].reshape(band_rows * breadth, features).astype(jnp.float32)
        result = own_rows + jnp.dot(activated, w_project, preferred_element_type=jnp.float32) + b_project
        return result.astype(jnp.bfloat16).reshape(band_rows, breadth, features)
    return lax.map(one_band, jnp.arange(n_bands, dtype=jnp.int32)).reshape(height, breadth, features)

def reference(tokens, bn_scale, bn_shift, w_expand, b_expand, dw_kernel, dw_bias, w_project, b_project, norm_gains, attn_qkv, attn_out, rel_bias, mlp_up, mlp_down):
    height, breadth, features = tokens.shape
    position_index = table_index(WIN)
    after_conv = mbconv(tokens, bn_scale, bn_shift, w_expand, b_expand, dw_kernel, dw_bias, w_project, b_project)
    blocks = after_conv.reshape(height // WIN, WIN, breadth // WIN, WIN, features).transpose(0, 2, 1, 3, 4)
    blocks = blocks.reshape(-1, WIN * WIN, features)
    after_block = attend_all(blocks, norm_gains[0], attn_qkv[0], attn_out[0], rel_bias[0][:, position_index])
    after_block = after_block.reshape(height // WIN, breadth // WIN, WIN, WIN, features).transpose(0, 2, 1, 3, 4)
    after_mlp = mlp_all(after_block.reshape(-1, features), norm_gains[1], mlp_up[0], mlp_down[0])
    stride_r = height // GRID
    stride_c = breadth // GRID
    grids = after_mlp.reshape(GRID, stride_r, GRID, stride_c, features).transpose(1, 3, 0, 2, 4)
    grids = grids.reshape(-1, GRID * GRID, features)
    after_grid = attend_all(grids, norm_gains[2], attn_qkv[1], attn_out[1], rel_bias[1][:, position_index])
    after_grid = after_grid.reshape(stride_r, stride_c, GRID, GRID, features).transpose(2, 0, 3, 1, 4)
    block_out = mlp_all(after_grid.reshape(-1, features), norm_gains[3], mlp_up[1], mlp_down[1])
    return block_out.reshape(height, breadth, features)
```

```python
import functools
import math

import jax
import jax.numpy as jnp
from jax import lax
from jax.experimental import pallas as pl
from jax.experimental.pallas import tpu as pltpu
from jax.sharding import PartitionSpec as P

WIN = 8
BF = jnp.bfloat16
F32 = jnp.float32
MESH = pl.DeviceIdType.MESH


def gelu(v):
    half = v * 0.5
    inner = v * (0.7978845608 + 0.0356774081 * (v * v))
    return half + half * jnp.tanh(inner)


def dot(a, b):
    return jnp.dot(a, b, preferred_element_type=F32)


def layer_norm(x, gain):
    center = x - jnp.mean(x, axis=-1, keepdims=True)
    spread = jnp.mean(center * center, axis=-1, keepdims=True)
    return (center * lax.rsqrt(spread + 1e-05) * gain).astype(BF)


def attend_and_mlp(x, gain_a, gain_m, w_qkv, w_out, bias, w_up, w_down, head_masks, n_windows):
    qkv = dot(layer_norm(x, gain_a), w_qkv[...])
    q = (qkv[:, :256] * (math.log2(math.e) / math.sqrt(32.0))).astype(BF)
    k = qkv[:, 256:512].astype(BF)
    v = qkv[:, 512:].astype(BF)
    low = lax.broadcasted_iota(jnp.int32, (64, 128), 1) < 64
    contexts = []
    for w in range(n_windows):
        rows = slice(64 * w, 64 * w + 64)
        halves = []
        for g in range(2):
            lanes = slice(128 * g, 128 * g + 128)
            kk, vv = k[rows, lanes], v[rows, lanes]
            k_diag = jnp.concatenate([kk * m for m in head_masks], axis=0)
            s = lax.dot_general(
                q[rows, lanes], k_diag, (((1,), (1,)), ((), ())), preferred_element_type=F32
            )
            s = s + bias[:, 256 * g : 256 * g + 256]
            probs = []
            for p in range(2):
                sp = s[:, 128 * p : 128 * p + 128]
                top_lo = jnp.max(jnp.where(low, sp, -jnp.inf), axis=-1, keepdims=True)
                top_hi = jnp.max(jnp.where(low, -jnp.inf, sp), axis=-1, keepdims=True)
                probs.append(jnp.exp2(sp - jnp.where(low, top_lo, top_hi)).astype(BF))
            p4 = jnp.concatenate(probs, axis=1)
            v_diag = jnp.concatenate(
                [jnp.concatenate([vv * m, m], axis=1) for m in head_masks], axis=0
            )
            o = dot(p4, v_diag)
            halves.append(o[:, :128] / o[:, 128:])
        contexts.append(jnp.concatenate(halves, axis=1).astype(BF))
    y = x + dot(jnp.concatenate(contexts, axis=0), w_out[...])
    h = gelu(dot(layer_norm(y, gain_m), w_up[...])).astype(BF)
    return y + dot(h, w_down[...])


def body(
    tokens,
    bn_scale,
    bn_shift,
    w_expand,
    b_expand,
    dw_taps,
    w_project,
    b_project,
    gains,
    w_qkv,
    w_out,
    bias,
    w_up,
    w_down,
    out,
    xf,
    hid,
    taps,
    act,
    conv,
    edge,
    halo_row,
    halo_col,
    halo_hid,
    send,
    recv,
    gathered,
    finished,
    ret,
    halo_send_sem,
    halo_recv_sem,
    go_send_sem,
    go_recv_sem,
    back_send_sem,
    back_recv_sem,
    own_sem,
):
    row = lax.axis_index("row")
    col = lax.axis_index("col")
    core = lax.rem(row, 2)
    pa = row // 2
    me = pa * 8 + col

    def device(index):
        return (2 * (index // 8) + core, lax.rem(index, 8))

    barrier = pltpu.get_barrier_semaphore()

    @pl.loop(1, 64)
    def _(step):
        to_row = 2 * lax.rem(pa + step // 8, 8) + core
        to_col = lax.rem(col + step, 8)
        pl.semaphore_signal(barrier, inc=1, device_id=(to_row, to_col), device_id_type=MESH)

    up, down = lax.rem(row + 15, 16), lax.rem(row + 1, 16)
    left, right = lax.rem(col + 7, 8), lax.rem(col + 1, 8)
    for r in (up, down):
        for c in (left, col, right):
            pl.semaphore_signal(barrier, inc=1, device_id=(r, c), device_id_type=MESH)

    def load_rows(source, at):
        for half in range(2):
            xf[half, pl.ds(pl.multiple_of(at * 256, 256), 256), :] = source[
                :, 128 * half : 128 * half + 128
            ].astype(F32)

    @pl.loop(0, 16)
    def _(r):
        load_rows(tokens[r], r)

    for side in range(2):
        column = [xf[half, pl.ds(255 * side, 16, stride=256), :] for half in range(2)]
        edge[side] = jnp.concatenate(column, axis=1).astype(BF)
    for t in range(10):
        taps[t] = jnp.broadcast_to(dw_taps[t : t + 1, :], (16, 1024)).astype(BF)

    pl.semaphore_wait(barrier, 69)

    halo_copies = []

    def send_halo(src, dst, to):
        n = len(halo_copies)
        copy = pltpu.make_async_remote_copy(
            src_ref=src,
            dst_ref=dst,
            send_sem=halo_send_sem.at[n],
            recv_sem=halo_recv_sem.at[n],
            device_id=to,
            device_id_type=MESH,
        )
        copy.start()
        halo_copies.append(copy)

    send_halo(tokens.at[0], halo_row.at[1], (up, col))
    send_halo(tokens.at[15], halo_row.at[0], (down, col))
    for r, slot in ((up, 2), (row, 1), (down, 0)):
        send_halo(edge.at[0], halo_col.at[1, slot], (r, left))
        send_halo(edge.at[1], halo_col.at[0, slot], (r, right))

    def permuted(at):
        return [
            jnp.concatenate(
                [xf[half, pl.ds(at * 256 + j, 16, stride=16), :] for half in range(2)], axis=1
            )
            for j in range(16)
        ]

    def expand(x, lanes):
        normed = (x * bn_scale[...] + bn_shift[...]).astype(BF)
        return gelu(dot(normed, w_expand[:, lanes]) + b_expand[:, lanes])

    def hidden_row(source, at, mask):
        x = jnp.concatenate(permuted(source), axis=0)
        for n in range(4):
            lanes = slice(256 * n, 256 * n + 256)
            h = expand(x, lanes)
            if mask is not None:
                h = h * mask
            hid[at, 1:17, :, lanes] = h.astype(BF).reshape(16, 16, 256)
            hid[at, 0, :, lanes] = pltpu.roll(h[240:, :], 1, 0).astype(BF)
            hid[at, 17, :, lanes] = pltpu.roll(h[:16, :], 15, 0).astype(BF)

    @pl.loop(0, 16)
    def _(r):
        hidden_row(r, r + 1, None)

    for copy in halo_copies:
        copy.wait()

    top = jnp.where(row > 0, 1.0, 0.0).astype(F32)
    bottom = jnp.where(row < 15, 1.0, 0.0).astype(F32)
    for slot, mask in ((0, top), (1, bottom)):
        load_rows(halo_row[slot], 16 + slot)
        hidden_row(16 + slot, 17 * slot, mask)
    for side, inside in ((0, col > 0), (1, col < 7)):
        x = halo_col[side].reshape(48, 256).astype(F32)
        h = expand(x, slice(0, 1024)) * jnp.where(inside, 1.0, 0.0).astype(F32)
        halo_hid[side] = h
    place = lax.broadcasted_iota(jnp.int32, (16, 1024), 0)

    @pl.loop(0, 18)
    def _(r):
        inside = jnp.where(r == 0, top, jnp.where(r == 17, bottom, 1.0))
        for side in range(2):
            beside = halo_hid[side, pl.ds(15 + r, 1), :] * inside
            old = hid[r, 17 * side].astype(F32)
            hid[r, 17 * side] = jnp.where(place == 15 * side, beside, old).astype(BF)

    lane = lax.broadcasted_iota(jnp.int32, (64, 128), 1) // 32
    head_masks = [jnp.where(lane == h, 1.0, 0.0).astype(BF) for h in range(4)]

    def section(x, i, n_windows):
        return attend_and_mlp(
            x,
            gains[2 * i : 2 * i + 1, :],
            gains[2 * i + 1 : 2 * i + 2, :],
            w_qkv.at[i],
            w_out.at[i],
            bias.at[i],
            w_up.at[i],
            w_down.at[i],
            head_masks,
            n_windows,
        )

    @pl.loop(0, 2)
    def _(band):
        @pl.loop(0, 8)
        def _(r):
            for n in range(8):
                lanes = slice(128 * n, 128 * n + 128)
                weights = [taps[t, :, lanes] for t in range(10)]
                for j in range(16):
                    total = weights[9]
                    for a in range(3):
                        for b in range(3):
                            total = total + hid[band * 8 + r + a, j + b, :, lanes] * weights[3 * a + b]
                    act[16 * j : 16 * j + 16, lanes] = gelu(total.astype(F32)).astype(BF)
            x = jnp.concatenate(permuted(band * 8 + r), axis=0)
            y = x + dot(act[...], w_project[...]) + b_project[...]
            for half in range(2):
                conv[half, pl.ds(pl.multiple_of(r * 256, 256), 256), :] = y[
                    :, 128 * half : 128 * half + 128
                ]

        @pl.loop(0, 8)
        def _(g):
            part = band * 2 + g // 4
            pieces = []
            for s in range(2):
                for jb in range(2):
                    for r in range(8):
                        start = r * 256 + jb * 128 + g * 2 + s
                        pieces.append(
                            jnp.concatenate(
                                [conv[half, pl.ds(start, 8, stride=16), :] for half in range(2)],
                                axis=1,
                            )
                        )
            y = section(jnp.concatenate(pieces, axis=0), 0, 4)
            within = lax.rem(g, 4) * 2
            for s in range(2):
                for r in range(8):
                    at = 128 * s + 8 * r
                    unit = jnp.concatenate([y[at : at + 8], y[at + 64 : at + 72]], axis=0)
                    send[part, r * 8 + within + s] = unit.astype(BF)

            @pl.loop(0, 16)
            def _(u):
                owner = (u // 2) * 8 + within + lax.rem(u, 2)

                @pl.when(owner != me)
                def _():
                    pltpu.make_async_remote_copy(
                        src_ref=send.at[part, owner],
                        dst_ref=recv.at[part, me],
                        send_sem=go_send_sem.at[part],
                        recv_sem=go_recv_sem.at[part],
                        device_id=device(owner),
                        device_id_type=MESH,
                    ).start()

                @pl.when(owner == me)
                def _():
                    recv[part, me] = send[part, owner]

    @pl.loop(0, 4)
    def _(part):
        others = recv.at[part, pl.ds(0, 63)]
        pltpu.make_async_copy(others, others, go_recv_sem.at[part]).wait()

        @pl.loop(0, 4)
        def _(piece):
            block = recv[part, pl.ds(piece * 16, 16)].reshape(256, 256)
            for half in range(2):
                gathered[half, pl.ds(pl.multiple_of(piece * 256, 256), 256), :] = block[
                    :, 128 * half : 128 * half + 128
                ].astype(F32)

        @pl.loop(0, 4)
        def _(g):
            windows = [
                jnp.concatenate(
                    [gathered[half, pl.ds(g * 4 + t, 64, stride=16), :] for half in range(2)], axis=1
                )
                for t in range(4)
            ]
            y = section(jnp.concatenate(windows, axis=0), 1, 4)
            for half in range(2):
                finished[half, pl.ds(pl.multiple_of(g * 256, 256), 256), :] = y[
                    :, 128 * half : 128 * half + 128
                ]

        out_row = (part // 2) * 8 + me // 8
        out_col = pl.multiple_of(lax.rem(part, 2) * 128 + lax.rem(me, 8) * 16, 16)

        @pl.loop(0, 64)
        def _(source):
            unit = [finished[half, pl.ds(source, 16, stride=64), :] for half in range(2)]
            ret[part, source] = jnp.concatenate(unit, axis=1).astype(BF)

            @pl.when(source != me)
            def _():
                pltpu.make_async_remote_copy(
                    src_ref=ret.at[part, source],
                    dst_ref=out.at[out_row, pl.ds(out_col, 16)],
                    send_sem=back_send_sem.at[part],
                    recv_sem=back_recv_sem.at[part],
                    device_id=device(source),
                    device_id_type=MESH,
                ).start()

            @pl.when(source == me)
            def _():
                pltpu.make_async_copy(
                    ret.at[part, source],
                    out.at[out_row, pl.ds(out_col, 16)],
                    own_sem.at[part],
                ).start()

    @pl.loop(0, 4)
    def _(part):
        sent = send.at[part, pl.ds(0, 63)]
        pltpu.make_async_copy(sent, sent, go_send_sem.at[part]).wait()
        back = ret.at[part, pl.ds(0, 63)]
        pltpu.make_async_copy(back, back, back_send_sem.at[part]).wait()
        pltpu.make_async_copy(back, back, back_recv_sem.at[part]).wait()
        pltpu.make_async_copy(ret.at[part, 0], ret.at[part, 0], own_sem.at[part]).wait()


def table_index(window):
    places = jnp.arange(window * window, dtype=jnp.int32)
    across = places // window
    within = places % window
    row_part = (across[:, None] - across[None, :] + window - 1) * (2 * window - 1)
    return row_part + (within[:, None] - within[None, :] + window - 1)


def bias_tables(rel_bias):
    sections, heads, entries = rel_bias.shape
    index = table_index(WIN).reshape(1, -1)
    onehot = (jnp.arange(entries, dtype=jnp.int32)[:, None] == index).astype(F32)
    lookup = jnp.dot(
        rel_bias.reshape(-1, entries) * math.log2(math.e), onehot, precision=lax.Precision.HIGHEST
    )
    lookup = lookup.reshape(sections, heads, 64, 64).transpose(0, 2, 1, 3)
    return lookup.reshape(sections, 64, heads * 64)


def on_device(
    tokens,
    bn_scale,
    bn_shift,
    w_expand,
    b_expand,
    dw_kernel,
    dw_bias,
    w_project,
    b_project,
    norm_gains,
    attn_qkv,
    attn_out,
    rel_bias,
    mlp_up,
    mlp_down,
):
    dw_taps = jnp.concatenate([dw_kernel.reshape(9, 1024), dw_bias.reshape(1, 1024)], axis=0)
    vmem = pl.BlockSpec(memory_space=pltpu.VMEM)
    return pl.pallas_call(
        body,
        out_shape=jax.ShapeDtypeStruct((16, 256, 256), BF),
        in_specs=[vmem] * 14,
        out_specs=pl.BlockSpec(memory_space=pl.ANY),
        scratch_shapes=[
            pltpu.VMEM((2, 18 * 256, 128), F32),
            pltpu.VMEM((18, 18, 16, 1024), BF),
            pltpu.VMEM((10, 16, 1024), BF),
            pltpu.VMEM((256, 1024), BF),
            pltpu.VMEM((2, 8 * 256, 128), F32),
            pltpu.VMEM((2, 16, 256), BF),
            pltpu.VMEM((2, 256, 256), BF),
            pltpu.VMEM((2, 3, 16, 256), BF),
            pltpu.VMEM((2, 48, 1024), F32),
            pltpu.VMEM((4, 64, 16, 256), BF),
            pltpu.VMEM((4, 64, 16, 256), BF),
            pltpu.VMEM((2, 1024, 128), F32),
            pltpu.VMEM((2, 1024, 128), F32),
            pltpu.VMEM((4, 64, 16, 256), BF),
            pltpu.SemaphoreType.DMA((8,)),
            pltpu.SemaphoreType.DMA((8,)),
            pltpu.SemaphoreType.DMA((4,)),
            pltpu.SemaphoreType.DMA((4,)),
            pltpu.SemaphoreType.DMA((4,)),
            pltpu.SemaphoreType.DMA((4,)),
            pltpu.SemaphoreType.DMA((4,)),
        ],
        compiler_params=pltpu.CompilerParams(
            collective_id=0, has_side_effects=True, vmem_limit_bytes=56 * 1024 * 1024
        ),
        cost_estimate=pl.CostEstimate(
            flops=20_000_000_000, bytes_accessed=8_000_000, transcendentals=20_000_000
        ),
        name="maxvit",
    )(
        tokens,
        bn_scale.reshape(1, -1),
        bn_shift.reshape(1, -1),
        w_expand,
        b_expand.reshape(1, -1),
        dw_taps,
        w_project,
        b_project.reshape(1, -1),
        norm_gains,
        attn_qkv,
        attn_out,
        bias_tables(rel_bias),
        mlp_up,
        mlp_down,
    )


def solution(mesh):
    placed = (P("row", "col", None),) + (P(),) * 14
    return jax.shard_map(
        on_device, mesh=mesh, in_specs=placed, out_specs=P("row", "col", None), check_vma=False
    )
```

```python
import math

import jax
import jax.numpy as jnp
from jax import lax
from jax.experimental import pallas as pl
from jax.experimental.pallas import tpu as pltpu
from jax.sharding import PartitionSpec as P

WIN = 8
BF = jnp.bfloat16
F32 = jnp.float32
MESH = pl.DeviceIdType.MESH


def gelu_of_half(h):
    h = h.astype(BF)
    inner = h * (BF(2 * 0.7978845608) + BF(8 * 0.0356774081) * (h * h))
    return h + h * jnp.tanh(inner)


def dot(a, b):
    return jnp.dot(a, b, preferred_element_type=F32)


def layer_norm(x, gain):
    center = x - jnp.mean(x, axis=-1, keepdims=True)
    spread = jnp.mean(center * center, axis=-1, keepdims=True)
    return (center * lax.rsqrt(spread + 1e-05) * gain).astype(BF)


def attend(x, gain, w_qkv, w_out, bias, head_masks):
    qkv = dot(layer_norm(x, gain), w_qkv[...])
    q = (qkv[:, :256] * (math.log2(math.e) / math.sqrt(32.0))).astype(BF)
    k = qkv[:, 256:512].astype(BF)
    v = qkv[:, 512:].astype(BF)
    low = lax.broadcasted_iota(jnp.int32, (64, 128), 1) < 64
    contexts = []
    for w in range(x.shape[0] // 64):
        rows = slice(64 * w, 64 * w + 64)
        halves = []
        for g in range(2):
            lanes = slice(128 * g, 128 * g + 128)
            kk, vv = k[rows, lanes], v[rows, lanes]
            k_diag = jnp.concatenate([kk * m for m in head_masks], axis=0)
            s = lax.dot_general(
                q[rows, lanes], k_diag, (((1,), (1,)), ((), ())), preferred_element_type=F32
            )
            s = s + bias[:, 256 * g : 256 * g + 256]
            probs = []
            for p in range(2):
                sp = s[:, 128 * p : 128 * p + 128]
                top_lo = jnp.max(jnp.where(low, sp, -jnp.inf), axis=-1, keepdims=True)
                top_hi = jnp.max(jnp.where(low, -jnp.inf, sp), axis=-1, keepdims=True)
                probs.append(jnp.exp2(sp - jnp.where(low, top_lo, top_hi)).astype(BF))
            p4 = jnp.concatenate(probs, axis=1)
            v_diag = jnp.concatenate(
                [jnp.concatenate([vv * m, m], axis=1) for m in head_masks], axis=0
            )
            o = dot(p4, v_diag)
            halves.append(o[:, :128] / o[:, 128:])
        contexts.append(jnp.concatenate(halves, axis=1).astype(BF))
    return x + dot(jnp.concatenate(contexts, axis=0), w_out[...])


def mlp(y, gain, w_up, w_down):
    h = gelu_of_half(dot(layer_norm(y, gain * 0.5), w_up[...]))
    return y + dot(h, w_down[...])


def fill_bias(rel_bias, split, looked_up, bias):
    rest = rel_bias[...] * math.log2(math.e)
    split[...] = jnp.zeros_like(split)
    for n in range(3):
        piece = rest.astype(BF)
        rest = rest - piece.astype(F32)
        split[16 * n : 16 * n + 16, :225] = piece.astype(F32)
    lane = lax.broadcasted_iota(jnp.int32, (1, 4096), 1)
    q = lax.rem(lane // 64, 2) * 32 + lane // 128
    k = lax.rem(lane, 64)
    entry = (q // 8 - k // 8 + 7) * 15 + lax.rem(q, 8) - lax.rem(k, 8) + 7
    onehot = jnp.where(lax.broadcasted_iota(jnp.int32, (256, 4096), 0) == entry, 1.0, 0.0)
    found = dot(split[...].astype(BF), onehot.astype(BF))
    found = found[:16] + found[16:32] + found[32:]
    for t in range(32):
        looked_up[16 * t : 16 * t + 16, :] = found[:, 128 * t : 128 * t + 128]
    low = lax.broadcasted_iota(jnp.int32, (32, 128), 1) < 64
    for i in range(2):
        for pair in range(4):
            even = looked_up[pl.ds(8 * i + 2 * pair, 32, stride=16), :]
            odd = looked_up[pl.ds(8 * i + 2 * pair + 1, 32, stride=16), :]
            lanes = slice(128 * pair, 128 * pair + 128)
            bias[i, :32, lanes] = jnp.where(low, even, pltpu.roll(odd, 64, 1))
            bias[i, 32:, lanes] = jnp.where(low, pltpu.roll(even, 64, 1), odd)


def body(
    tokens,
    bn_scale,
    bn_shift,
    w_expand,
    b_expand,
    dw_kernel,
    dw_bias,
    w_project,
    b_project,
    gains,
    w_qkv,
    w_out,
    rel_bias,
    w_up,
    w_down,
    out,
    xf,
    hid,
    taps,
    act,
    conv,
    edge,
    halo_row,
    halo_col,
    halo_hid,
    split,
    looked_up,
    bias,
    send,
    recv,
    gathered,
    finished,
    ret,
    back,
    done,
    halo_send_sem,
    halo_recv_sem,
    go_send_sem,
    go_recv_sem,
    back_send_sem,
    back_recv_sem,
    out_sem,
):
    row = lax.axis_index("row")
    col = lax.axis_index("col")
    core = lax.rem(row, 2)
    pa = row // 2
    me = pa * 8 + col

    def device(index):
        return (2 * (index // 8) + core, lax.rem(index, 8))

    barrier = pltpu.get_barrier_semaphore()

    @pl.loop(1, 64)
    def _(step):
        pl.semaphore_signal(
            barrier, inc=1, device_id=device(lax.rem(me + step, 64)), device_id_type=MESH
        )

    up, down = lax.rem(row + 15, 16), lax.rem(row + 1, 16)
    left, right = lax.rem(col + 7, 8), lax.rem(col + 1, 8)
    for r in (up, down):
        for c in (left, col, right):
            pl.semaphore_signal(barrier, inc=1, device_id=(r, c), device_id_type=MESH)

    def load_rows(source, at):
        for half in range(2):
            xf[half, pl.ds(pl.multiple_of(at * 256, 256), 256), :] = source[
                :, 128 * half : 128 * half + 128
            ].astype(F32)

    @pl.loop(0, 16)
    def _(r):
        load_rows(tokens[r], r)

    for side in range(2):
        column = [xf[half, pl.ds(255 * side, 16, stride=256), :] for half in range(2)]
        edge[side] = jnp.concatenate(column, axis=1).astype(BF)
    for t in range(9):
        tap = dw_kernel[t // 3, t % 3 : t % 3 + 1, :]
        taps[t] = jnp.broadcast_to(tap * 0.5, (16, 1024)).astype(BF)
    taps[9] = jnp.broadcast_to(dw_bias[...] * 0.5, (16, 1024)).astype(BF)

    pl.semaphore_wait(barrier, 69)

    halo_copies = []

    def send_halo(src, dst, to):
        n = len(halo_copies)
        copy = pltpu.make_async_remote_copy(
            src_ref=src,
            dst_ref=dst,
            send_sem=halo_send_sem.at[n],
            recv_sem=halo_recv_sem.at[n],
            device_id=to,
            device_id_type=MESH,
        )
        copy.start()
        halo_copies.append(copy)

    send_halo(tokens.at[0], halo_row.at[1], (up, col))
    send_halo(tokens.at[15], halo_row.at[0], (down, col))
    for r, slot in ((up, 2), (row, 1), (down, 0)):
        send_halo(edge.at[0], halo_col.at[1, slot], (r, left))
        send_halo(edge.at[1], halo_col.at[0, slot], (r, right))

    def normed_half(x):
        return (x * (bn_scale[...] * 0.5) + bn_shift[...] * 0.5).astype(BF)

    def expand(normed, lanes):
        return gelu_of_half(dot(normed, w_expand[:, lanes]) + b_expand[:, lanes] * 0.5)

    def hidden_rows(source, at, masks):
        count = len(masks)
        x = [
            jnp.concatenate(
                [xf[half, pl.ds((source + i) * 256 + j, 32, stride=8), :] for half in range(2)],
                axis=1,
            )
            for i in range(count)
            for j in range(8)
        ]
        normed = normed_half(jnp.concatenate(x, axis=0))
        for n in range(4):
            lanes = slice(256 * n, 256 * n + 256)
            rows = expand(normed, lanes)
            for i, mask in enumerate(masks):
                h = rows[256 * i : 256 * i + 256]
                if mask is not None:
                    h = h * mask
                hid[at + i, 1:9, :, lanes] = h.reshape(8, 32, 256)
                first, last = h[:32].astype(F32), h[224:].astype(F32)
                hid[at + i, 0, :, lanes] = pltpu.roll(last, 1, 0).astype(BF)
                hid[at + i, 9, :, lanes] = pltpu.roll(first, 31, 0).astype(BF)

    top = jnp.where(row > 0, 1.0, 0.0).astype(F32)
    bottom = jnp.where(row < 15, 1.0, 0.0).astype(F32)
    place = lax.broadcasted_iota(jnp.int32, (16, 1024), 0)

    def place_edges(r):
        inside = jnp.where(r == 0, top, jnp.where(r == 17, bottom, 1.0))
        for side in range(2):
            beside = halo_hid[side, pl.ds(15 + r, 1), :] * inside
            rows = slice(16 * side, 16 * side + 16)
            old = hid[r, 9 * side, rows].astype(F32)
            hid[r, 9 * side, rows] = jnp.where(place == 15 * side, beside, old).astype(BF)

    fill_bias(rel_bias, split, looked_up, bias)

    @pl.loop(0, 3)
    def _(r):
        hidden_rows(r * 3, r * 3 + 1, [None] * 3)

    for copy in halo_copies:
        copy.wait()

    load_rows(halo_row[1], 16)
    load_rows(halo_row[0], 17)
    hidden_rows(17, 0, [top.astype(BF)])
    for side, inside in ((0, col > 0), (1, col < 7)):
        x = halo_col[side].reshape(48, 256).astype(F32)
        h = expand(normed_half(x), slice(0, 1024)).astype(F32)
        halo_hid[side] = h * jnp.where(inside, 1.0, 0.0).astype(F32)
    pl.loop(0, 10)(place_edges)

    lane = lax.broadcasted_iota(jnp.int32, (64, 128), 1) // 32
    head_masks = [jnp.where(lane == h, 1.0, 0.0).astype(BF) for h in range(4)]

    x_chip, y_chip, z_chip = (col // 4) * 2 + lax.rem(pa, 2), pa // 2, lax.rem(col, 4)

    def push_units(part, source, target, send_sem, recv_sem):
        def push(to_pa, to_x, to_z):
            to_col = (to_x // 2) * 4 + to_z
            pltpu.make_async_remote_copy(
                src_ref=source.at[part, to_pa * 8 + to_col],
                dst_ref=target.at[part, me],
                send_sem=send_sem.at[part],
                recv_sem=recv_sem.at[part],
                device_id=(2 * to_pa + core, to_col),
                device_id_type=MESH,
            ).start()

        to_z = [lax.rem(z_chip + b, 4) for b in range(4)]

        def push_group(a, skip):
            to_y = lax.rem(y_chip + a // 2, 4)
            to_x = lax.rem(x_chip + lax.rem(a, 2), 4)
            opposite = lax.rem(to_x + 2, 4)
            to_pa = to_y * 2 + lax.rem(to_x, 2)
            for b in range(skip, 8):
                push(to_pa, to_x if b < 4 else opposite, to_z[b % 4])

        push_group(0, 1)
        pl.loop(1, 8)(lambda a: push_group(a, 0))

    def conv_part(band, side):
        columns = pl.ds(pl.multiple_of(side * 16, 16), 16)

        @pl.loop(0, 4)
        def _(pair):
            for n in range(8):
                lanes = slice(128 * n, 128 * n + 128)
                weights = [taps[t, :, lanes] for t in range(10)]
                window = [
                    [hid[band * 8 + pair * 2 + a, j, columns, lanes] for a in range(4)]
                    for j in range(10)
                ]
                results = []
                for j in range(8):
                    for i in range(2):
                        total = weights[9]
                        for b in range(3):
                            for a in range(3):
                                total = total + window[j + b][i + a] * weights[3 * a + b]
                        results.append(gelu_of_half(total))
                for j in range(8):
                    for i in range(2):
                        at = pl.multiple_of(pair * 256 + i * 128 + j * 16, 16)
                        act[pl.ds(at, 16), lanes] = results[2 * j + i]

        x = [
            jnp.concatenate(
                [
                    xf[half, pl.ds((band * 8 + r) * 256 + side * 128 + j, 16, stride=8), :]
                    for half in range(2)
                ],
                axis=1,
            )
            for r in range(8)
            for j in range(8)
        ]
        y = jnp.concatenate(x, axis=0) + dot(act[...], w_project[...]) + b_project[...]
        for half in range(2):
            conv[half, :, :] = y[:, 128 * half : 128 * half + 128]

    def block_part(part):
        pieces = [
            jnp.concatenate(
                [conv[half, pl.ds(r * 128 + s, 8, stride=16), :] for half in range(2)], axis=1
            )
            for s in range(16)
            for r in range(8)
        ]
        y = attend(
            jnp.concatenate(pieces, axis=0),
            gains[0:1, :],
            w_qkv.at[0],
            w_out.at[0],
            bias.at[0],
            head_masks,
        )
        y = mlp(y, gains[1:2, :], w_up.at[0], w_down.at[0])
        for s in range(8):
            for r in range(8):
                at = 128 * s + 8 * r
                unit = jnp.concatenate([y[at : at + 8], y[at + 64 : at + 72]], axis=0)
                send[part, r * 8 + s] = unit.astype(BF)

        push_units(part, send, recv, go_send_sem, go_recv_sem)

        recv[part, me] = send[part, me]

    def grid_part(part):
        others = recv.at[part, pl.ds(0, 63)]
        pltpu.make_async_copy(others, others, go_recv_sem.at[part]).wait()

        @pl.loop(0, 4)
        def _(piece):
            block = recv[part, pl.ds(piece * 16, 16)].reshape(256, 256)
            for half in range(2):
                gathered[half, pl.ds(pl.multiple_of(piece * 256, 256), 256), :] = block[
                    :, 128 * half : 128 * half + 128
                ].astype(F32)

        windows = [
            jnp.concatenate([gathered[half, pl.ds(t, 64, stride=16), :] for half in range(2)], axis=1)
            for t in range(16)
        ]
        y = attend(
            jnp.concatenate(windows, axis=0),
            gains[2:3, :],
            w_qkv.at[1],
            w_out.at[1],
            bias.at[1],
            head_masks,
        )
        for half in range(2):
            finished[half, :, :] = y[:, 128 * half : 128 * half + 128]
        for source in range(64):
            unit = [finished[half, pl.ds(source, 16, stride=64), :] for half in range(2)]
            ret[part, source] = jnp.concatenate(unit, axis=1).astype(BF)

        push_units(part, ret, back, back_send_sem, back_recv_sem)

        back[part, me] = ret[part, me]

    @pl.loop(0, 5)
    def _(step):
        @pl.when(step == 2)
        def _():
            @pl.loop(0, 2)
            def _(r):
                hidden_rows(r * 3 + 9, r * 3 + 10, [None] * 3)

            hidden_rows(15, 16, [None, bottom.astype(BF)])
            pl.loop(10, 18)(place_edges)

        @pl.when(step < 4)
        def _():
            conv_part(step // 2, lax.rem(step, 2))
            block_part(step)

        @pl.when(step >= 1)
        def _():
            grid_part(step - 1)

    def store(part):
        return pltpu.make_async_copy(
            done.at[part],
            out.at[
                pl.ds((part // 2) * 8, 8), pl.ds(pl.multiple_of(lax.rem(part, 2) * 128, 128), 128)
            ],
            out_sem.at[part],
        )

    @pl.loop(0, 4)
    def _(part):
        others = back.at[part, pl.ds(0, 63)]
        pltpu.make_async_copy(others, others, back_recv_sem.at[part]).wait()
        y = back[part].reshape(1024, 256).astype(F32)
        y = mlp(y, gains[3:4, :], w_up.at[1], w_down.at[1])
        done[part] = y.astype(BF).reshape(8, 128, 256)
        store(part).start()

    @pl.loop(0, 4)
    def _(part):
        sent = send.at[part, pl.ds(0, 63)]
        pltpu.make_async_copy(sent, sent, go_send_sem.at[part]).wait()
        returned = ret.at[part, pl.ds(0, 63)]
        pltpu.make_async_copy(returned, returned, back_send_sem.at[part]).wait()
        store(part).wait()


def on_device(
    tokens,
    bn_scale,
    bn_shift,
    w_expand,
    b_expand,
    dw_kernel,
    dw_bias,
    w_project,
    b_project,
    norm_gains,
    attn_qkv,
    attn_out,
    rel_bias,
    mlp_up,
    mlp_down,
):
    vmem = pl.BlockSpec(memory_space=pltpu.VMEM)
    units = pltpu.VMEM((4, 64, 16, 256), BF)
    return pl.pallas_call(
        body,
        out_shape=jax.ShapeDtypeStruct((16, 256, 256), BF),
        in_specs=[vmem] * 15,
        out_specs=pl.BlockSpec(memory_space=pl.ANY),
        scratch_shapes=[
            pltpu.VMEM((2, 18 * 256, 128), F32),
            pltpu.VMEM((18, 10, 32, 1024), BF),
            pltpu.VMEM((10, 16, 1024), BF),
            pltpu.VMEM((1024, 1024), BF),
            pltpu.VMEM((2, 1024, 128), F32),
            pltpu.VMEM((2, 16, 256), BF),
            pltpu.VMEM((2, 256, 256), BF),
            pltpu.VMEM((2, 3, 16, 256), BF),
            pltpu.VMEM((2, 48, 1024), F32),
            pltpu.VMEM((48, 256), F32),
            pltpu.VMEM((512, 128), F32),
            pltpu.VMEM((2, 64, 512), F32),
            units,
            units,
            pltpu.VMEM((2, 1024, 128), F32),
            pltpu.VMEM((2, 1024, 128), F32),
            units,
            units,
            pltpu.VMEM((4, 8, 128, 256), BF),
            pltpu.SemaphoreType.DMA((8,)),
            pltpu.SemaphoreType.DMA((8,)),
            pltpu.SemaphoreType.DMA((4,)),
            pltpu.SemaphoreType.DMA((4,)),
            pltpu.SemaphoreType.DMA((4,)),
            pltpu.SemaphoreType.DMA((4,)),
            pltpu.SemaphoreType.DMA((4,)),
        ],
        compiler_params=pltpu.CompilerParams(
            collective_id=0, has_side_effects=True, vmem_limit_bytes=60 * 1024 * 1024
        ),
        cost_estimate=pl.CostEstimate(
            flops=20_000_000_000, bytes_accessed=8_000_000, transcendentals=20_000_000
        ),
        name="maxvit",
    )(
        tokens,
        bn_scale.reshape(1, -1),
        bn_shift.reshape(1, -1),
        w_expand,
        b_expand.reshape(1, -1),
        dw_kernel,
        dw_bias.reshape(1, -1),
        w_project,
        b_project.reshape(1, -1),
        norm_gains,
        attn_qkv,
        attn_out,
        rel_bias.reshape(16, 225),
        mlp_up,
        mlp_down,
    )


def solution(mesh):
    placed = (P("row", "col", None),) + (P(),) * 14
    return jax.shard_map(
        on_device, mesh=mesh, in_specs=placed, out_specs=P("row", "col", None), check_vma=False
    )
```

```python
import math

import jax
import jax.numpy as jnp
from jax import lax
from jax.experimental import pallas as pl
from jax.experimental.pallas import tpu as pltpu
from jax.sharding import PartitionSpec as P

WIN = 8
BF = jnp.bfloat16
F32 = jnp.float32
MESH = pl.DeviceIdType.MESH


def gelu_of_half(h):
    h = h.astype(BF)
    inner = h * (BF(2 * 0.7978845608) + BF(8 * 0.0356774081) * (h * h))
    return h + h * jnp.tanh(inner)


def dot(a, b):
    return jnp.dot(a, b, preferred_element_type=F32)


def layer_norm(x, gain):
    center = x - jnp.mean(x, axis=-1, keepdims=True)
    spread = jnp.mean(center * center, axis=-1, keepdims=True)
    return (center * lax.rsqrt(spread + 1e-05) * gain).astype(BF)


def attend(x, gain, w_qkv, w_out, bias, head_masks):
    qkv = dot(layer_norm(x, gain), w_qkv[...])
    q = (qkv[:, :256] * (math.log2(math.e) / math.sqrt(32.0))).astype(BF)
    k = qkv[:, 256:512].astype(BF)
    v = qkv[:, 512:].astype(BF)
    low = lax.broadcasted_iota(jnp.int32, (64, 128), 1) < 64
    n_windows = x.shape[0] // 64
    pairs = [(w, g) for w in range(n_windows) for g in range(2)]

    def scores(w, g):
        rows, lanes = slice(64 * w, 64 * w + 64), slice(128 * g, 128 * g + 128)
        kk = k[rows, lanes]
        k_diag = jnp.concatenate([kk * m for m in head_masks], axis=0)
        return lax.dot_general(
            q[rows, lanes], k_diag, (((1,), (1,)), ((), ())), preferred_element_type=F32
        )

    def probabilities(s, g):
        s = s + bias[:, 256 * g : 256 * g + 256]
        probs = []
        for p in range(2):
            sp = s[:, 128 * p : 128 * p + 128]
            top_lo = jnp.max(jnp.where(low, sp, -jnp.inf), axis=-1, keepdims=True)
            top_hi = jnp.max(jnp.where(low, -jnp.inf, sp), axis=-1, keepdims=True)
            probs.append(jnp.exp2(sp - jnp.where(low, top_lo, top_hi)).astype(BF))
        return jnp.concatenate(probs, axis=1)

    def context(p4, w, g):
        vv = v[64 * w : 64 * w + 64, 128 * g : 128 * g + 128]
        v_diag = jnp.concatenate([jnp.concatenate([vv * m, m], axis=1) for m in head_masks], axis=0)
        o = dot(p4, v_diag)
        return (o[:, :128] / o[:, 128:]).astype(BF)

    found = [scores(w, g) for w, g in pairs]
    found = [probabilities(s, g) for s, (w, g) in zip(found, pairs)]
    halves = [context(p4, w, g) for p4, (w, g) in zip(found, pairs)]
    contexts = [
        jnp.concatenate(halves[2 * w : 2 * w + 2], axis=1) for w in range(n_windows)
    ]
    return x + dot(jnp.concatenate(contexts, axis=0), w_out[...])


def mlp(y, gain, w_up, w_down):
    h = gelu_of_half(dot(layer_norm(y, gain * 0.5), w_up[...]))
    return y + dot(h, w_down[...])


def fill_bias(rel_bias, split, looked_up, bias):
    rest = rel_bias[...] * math.log2(math.e)
    split[...] = jnp.zeros_like(split)
    for n in range(3):
        piece = rest.astype(BF)
        rest = rest - piece.astype(F32)
        split[16 * n : 16 * n + 16, :225] = piece.astype(F32)
    lane = lax.broadcasted_iota(jnp.int32, (1, 4096), 1)
    q = lax.rem(lane // 64, 2) * 32 + lane // 128
    k = lax.rem(lane, 64)
    entry = (q // 8 - k // 8 + 7) * 15 + lax.rem(q, 8) - lax.rem(k, 8) + 7
    onehot = jnp.where(lax.broadcasted_iota(jnp.int32, (256, 4096), 0) == entry, 1.0, 0.0)
    found = dot(split[...].astype(BF), onehot.astype(BF))
    found = found[:16] + found[16:32] + found[32:]
    for t in range(32):
        looked_up[16 * t : 16 * t + 16, :] = found[:, 128 * t : 128 * t + 128]
    low = lax.broadcasted_iota(jnp.int32, (32, 128), 1) < 64
    for i in range(2):
        for pair in range(4):
            even = looked_up[pl.ds(8 * i + 2 * pair, 32, stride=16), :]
            odd = looked_up[pl.ds(8 * i + 2 * pair + 1, 32, stride=16), :]
            lanes = slice(128 * pair, 128 * pair + 128)
            bias[i, :32, lanes] = jnp.where(low, even, pltpu.roll(odd, 64, 1))
            bias[i, 32:, lanes] = jnp.where(low, pltpu.roll(even, 64, 1), odd)


def body(
    tokens_hbm,
    bn_scale,
    bn_shift,
    w_expand_hbm,
    b_expand,
    dw_kernel,
    dw_bias,
    w_project_hbm,
    b_project,
    gains,
    w_qkv_hbm,
    w_out_hbm,
    rel_bias,
    w_up_hbm,
    w_down_hbm,
    out,
    tokens,
    w_expand,
    w_project,
    w_qkv,
    w_out,
    w_up,
    w_down,
    xf,
    hid,
    taps,
    act,
    conv,
    edge,
    halo_row,
    halo_col,
    halo_hid,
    split,
    looked_up,
    bias,
    send,
    recv,
    gathered,
    finished,
    ret,
    back,
    done,
    halo_send_sem,
    halo_recv_sem,
    go_send_sem,
    go_recv_sem,
    back_send_sem,
    back_recv_sem,
    out_sem,
    load_sem,
):
    row = lax.axis_index("row")
    col = lax.axis_index("col")
    core = lax.rem(row, 2)
    pa = row // 2
    me = pa * 8 + col

    def device(index):
        return (2 * (index // 8) + core, lax.rem(index, 8))

    loads = [
        pltpu.make_async_copy(source, target, load_sem.at[n])
        for n, (source, target) in enumerate(
            (
                (tokens_hbm, tokens),
                (w_expand_hbm, w_expand),
                (w_project_hbm, w_project),
                (w_qkv_hbm, w_qkv),
                (w_out_hbm, w_out),
                (w_up_hbm, w_up),
                (w_down_hbm, w_down),
            )
        )
    ]
    for load in loads:
        load.start()

    barrier = pltpu.get_barrier_semaphore()

    @pl.loop(1, 64)
    def _(step):
        pl.semaphore_signal(
            barrier, inc=1, device_id=device(lax.rem(me + step, 64)), device_id_type=MESH
        )

    up, down = lax.rem(row + 15, 16), lax.rem(row + 1, 16)
    left, right = lax.rem(col + 7, 8), lax.rem(col + 1, 8)
    for r in (up, down):
        for c in (left, col, right):
            pl.semaphore_signal(barrier, inc=1, device_id=(r, c), device_id_type=MESH)

    def load_rows(source, at):
        for half in range(2):
            xf[half, pl.ds(pl.multiple_of(at * 256, 256), 256), :] = source[
                :, 128 * half : 128 * half + 128
            ].astype(F32)

    loads[0].wait()

    @pl.loop(0, 16)
    def _(r):
        load_rows(tokens[r], r)

    for side in range(2):
        column = [xf[half, pl.ds(255 * side, 16, stride=256), :] for half in range(2)]
        edge[side] = jnp.concatenate(column, axis=1).astype(BF)
    for t in range(9):
        tap = dw_kernel[t // 3, t % 3 : t % 3 + 1, :]
        taps[t] = jnp.broadcast_to(tap * 0.5, (16, 1024)).astype(BF)
    taps[9] = jnp.broadcast_to(dw_bias[...] * 0.5, (16, 1024)).astype(BF)

    pl.semaphore_wait(barrier, 69)

    halo_copies = []

    def send_halo(src, dst, to):
        n = len(halo_copies)
        copy = pltpu.make_async_remote_copy(
            src_ref=src,
            dst_ref=dst,
            send_sem=halo_send_sem.at[n],
            recv_sem=halo_recv_sem.at[n],
            device_id=to,
            device_id_type=MESH,
        )
        copy.start()
        halo_copies.append(copy)

    send_halo(tokens.at[0], halo_row.at[1], (up, col))
    send_halo(tokens.at[15], halo_row.at[0], (down, col))
    for r, slot in ((up, 2), (row, 1), (down, 0)):
        send_halo(edge.at[0], halo_col.at[1, slot], (r, left))
        send_halo(edge.at[1], halo_col.at[0, slot], (r, right))

    def normed_half(x):
        return (x * (bn_scale[...] * 0.5) + bn_shift[...] * 0.5).astype(BF)

    def expand(normed, lanes):
        return gelu_of_half(dot(normed, w_expand[:, lanes]) + b_expand[:, lanes] * 0.5)

    def hidden_rows(source, at, masks):
        count = len(masks)
        x = [
            jnp.concatenate(
                [xf[half, pl.ds((source + i) * 256 + j, 32, stride=8), :] for half in range(2)],
                axis=1,
            )
            for i in range(count)
            for j in range(8)
        ]
        normed = normed_half(jnp.concatenate(x, axis=0))
        for n in range(4):
            lanes = slice(256 * n, 256 * n + 256)
            rows = expand(normed, lanes)
            for i, mask in enumerate(masks):
                h = rows[256 * i : 256 * i + 256]
                if mask is not None:
                    h = h * mask
                hid[at + i, 1:9, :, lanes] = h.reshape(8, 32, 256)
                first, last = h[:32].astype(F32), h[224:].astype(F32)
                hid[at + i, 0, :, lanes] = pltpu.roll(last, 1, 0).astype(BF)
                hid[at + i, 9, :, lanes] = pltpu.roll(first, 31, 0).astype(BF)

    top = jnp.where(row > 0, 1.0, 0.0).astype(F32)
    bottom = jnp.where(row < 15, 1.0, 0.0).astype(F32)
    place = lax.broadcasted_iota(jnp.int32, (16, 1024), 0)

    def place_edges(r):
        inside = jnp.where(r == 0, top, jnp.where(r == 17, bottom, 1.0))
        for side in range(2):
            beside = halo_hid[side, pl.ds(15 + r, 1), :] * inside
            rows = slice(16 * side, 16 * side + 16)
            old = hid[r, 9 * side, rows].astype(F32)
            hid[r, 9 * side, rows] = jnp.where(place == 15 * side, beside, old).astype(BF)

    fill_bias(rel_bias, split, looked_up, bias)
    loads[1].wait()

    @pl.loop(0, 5)
    def _(r):
        hidden_rows(r * 3, r * 3 + 1, [None] * 3)

    for copy in halo_copies:
        copy.wait()

    load_rows(halo_row[1], 16)
    load_rows(halo_row[0], 17)
    hidden_rows(17, 0, [top.astype(BF)])
    for side, inside in ((0, col > 0), (1, col < 7)):
        x = halo_col[side].reshape(48, 256).astype(F32)
        h = expand(normed_half(x), slice(0, 1024)).astype(F32)
        halo_hid[side] = h * jnp.where(inside, 1.0, 0.0).astype(F32)
    pl.loop(0, 10)(place_edges)

    lane = lax.broadcasted_iota(jnp.int32, (64, 128), 1) // 32
    head_masks = [jnp.where(lane == h, 1.0, 0.0).astype(BF) for h in range(4)]

    x_chip, y_chip, z_chip = (col // 4) * 2 + lax.rem(pa, 2), pa // 2, lax.rem(col, 4)

    def push_units(part, source, target, send_sem, recv_sem):
        def push(to_pa, to_x, to_z):
            to_col = (to_x // 2) * 4 + to_z
            pltpu.make_async_remote_copy(
                src_ref=source.at[part, to_pa * 8 + to_col],
                dst_ref=target.at[part, me],
                send_sem=send_sem.at[part],
                recv_sem=recv_sem.at[part],
                device_id=(2 * to_pa + core, to_col),
                device_id_type=MESH,
            ).start()

        to_z = [lax.rem(z_chip + b, 4) for b in range(4)]

        def push_group(a, skip):
            to_y = lax.rem(y_chip + a // 2, 4)
            to_x = lax.rem(x_chip + lax.rem(a, 2), 4)
            opposite = lax.rem(to_x + 2, 4)
            to_pa = to_y * 2 + lax.rem(to_x, 2)
            for b in range(skip, 8):
                push(to_pa, to_x if b < 4 else opposite, to_z[b % 4])

        push_group(0, 1)
        pl.loop(1, 8)(lambda a: push_group(a, 0))

    def conv_part(band, side):
        columns = pl.ds(pl.multiple_of(side * 16, 16), 16)

        @pl.loop(0, 4)
        def _(pair):
            for n in range(8):
                lanes = slice(128 * n, 128 * n + 128)
                weights = [taps[t, :, lanes] for t in range(10)]
                window = [
                    [hid[band * 8 + pair * 2 + a, j, columns, lanes] for a in range(4)]
                    for j in range(10)
                ]
                results = []
                for j in range(8):
                    for i in range(2):
                        total = weights[9]
                        for b in range(3):
                            for a in range(3):
                                total = total + window[j + b][i + a] * weights[3 * a + b]
                        results.append(gelu_of_half(total))
                for j in range(8):
                    for i in range(2):
                        at = pl.multiple_of(pair * 256 + i * 128 + j * 16, 16)
                        act[pl.ds(at, 16), lanes] = results[2 * j + i]

        x = [
            jnp.concatenate(
                [
                    xf[half, pl.ds((band * 8 + r) * 256 + side * 128 + j, 16, stride=8), :]
                    for half in range(2)
                ],
                axis=1,
            )
            for r in range(8)
            for j in range(8)
        ]
        y = jnp.concatenate(x, axis=0) + dot(act[...], w_project[...]) + b_project[...]
        for half in range(2):
            conv[half, :, :] = y[:, 128 * half : 128 * half + 128]

    def block_part(part):
        pieces = [
            jnp.concatenate(
                [conv[half, pl.ds(r * 128 + s, 8, stride=16), :] for half in range(2)], axis=1
            )
            for s in range(16)
            for r in range(8)
        ]
        y = attend(
            jnp.concatenate(pieces, axis=0),
            gains[0:1, :],
            w_qkv.at[0],
            w_out.at[0],
            bias.at[0],
            head_masks,
        )
        y = mlp(y, gains[1:2, :], w_up.at[0], w_down.at[0])
        for s in range(8):
            for r in range(8):
                at = 128 * s + 8 * r
                unit = jnp.concatenate([y[at : at + 8], y[at + 64 : at + 72]], axis=0)
                send[part, r * 8 + s] = unit.astype(BF)

        push_units(part, send, recv, go_send_sem, go_recv_sem)

        recv[part, me] = send[part, me]

    def grid_part(part):
        others = recv.at[part, pl.ds(0, 63)]
        pltpu.make_async_copy(others, others, go_recv_sem.at[part]).wait()

        @pl.loop(0, 4)
        def _(piece):
            block = recv[part, pl.ds(piece * 16, 16)].reshape(256, 256)
            for half in range(2):
                gathered[half, pl.ds(pl.multiple_of(piece * 256, 256), 256), :] = block[
                    :, 128 * half : 128 * half + 128
                ].astype(F32)

        windows = [
            jnp.concatenate([gathered[half, pl.ds(t, 64, stride=16), :] for half in range(2)], axis=1)
            for t in range(16)
        ]
        y = attend(
            jnp.concatenate(windows, axis=0),
            gains[2:3, :],
            w_qkv.at[1],
            w_out.at[1],
            bias.at[1],
            head_masks,
        )
        for half in range(2):
            finished[half, :, :] = y[:, 128 * half : 128 * half + 128]
        for source in range(64):
            unit = [finished[half, pl.ds(source, 16, stride=64), :] for half in range(2)]
            ret[part, source] = jnp.concatenate(unit, axis=1).astype(BF)

        push_units(part, ret, back, back_send_sem, back_recv_sem)

        back[part, me] = ret[part, me]

    for load in loads[2:]:
        load.wait()

    @pl.loop(0, 5)
    def _(step):
        @pl.when(step == 2)
        def _():
            hidden_rows(15, 16, [None, bottom.astype(BF)])
            pl.loop(10, 18)(place_edges)

        @pl.when(step < 4)
        def _():
            conv_part(step // 2, lax.rem(step, 2))
            block_part(step)

        @pl.when(step >= 1)
        def _():
            grid_part(step - 1)

    def store(part):
        return pltpu.make_async_copy(
            done.at[part],
            out.at[
                pl.ds((part // 2) * 8, 8), pl.ds(pl.multiple_of(lax.rem(part, 2) * 128, 128), 128)
            ],
            out_sem.at[part],
        )

    @pl.loop(0, 4)
    def _(part):
        others = back.at[part, pl.ds(0, 63)]
        pltpu.make_async_copy(others, others, back_recv_sem.at[part]).wait()
        y = back[part].reshape(1024, 256).astype(F32)
        y = mlp(y, gains[3:4, :], w_up.at[1], w_down.at[1])
        done[part] = y.astype(BF).reshape(8, 128, 256)
        store(part).start()

    @pl.loop(0, 4)
    def _(part):
        sent = send.at[part, pl.ds(0, 63)]
        pltpu.make_async_copy(sent, sent, go_send_sem.at[part]).wait()
        returned = ret.at[part, pl.ds(0, 63)]
        pltpu.make_async_copy(returned, returned, back_send_sem.at[part]).wait()
        store(part).wait()


def on_device(
    tokens,
    bn_scale,
    bn_shift,
    w_expand,
    b_expand,
    dw_kernel,
    dw_bias,
    w_project,
    b_project,
    norm_gains,
    attn_qkv,
    attn_out,
    rel_bias,
    mlp_up,
    mlp_down,
):
    vmem = pl.BlockSpec(memory_space=pltpu.VMEM)
    hbm = pl.BlockSpec(memory_space=pl.ANY)
    units = pltpu.VMEM((4, 64, 16, 256), BF)
    return pl.pallas_call(
        body,
        out_shape=jax.ShapeDtypeStruct((16, 256, 256), BF),
        in_specs=[hbm, vmem, vmem, hbm, vmem, vmem, vmem, hbm, vmem, vmem, hbm, hbm, vmem, hbm, hbm],
        out_specs=pl.BlockSpec(memory_space=pl.ANY),
        scratch_shapes=[
            pltpu.VMEM((16, 256, 256), BF),
            pltpu.VMEM((256, 1024), BF),
            pltpu.VMEM((1024, 256), BF),
            pltpu.VMEM((2, 256, 768), BF),
            pltpu.VMEM((2, 256, 256), BF),
            pltpu.VMEM((2, 256, 1024), BF),
            pltpu.VMEM((2, 1024, 256), BF),
            pltpu.VMEM((2, 18 * 256, 128), F32),
            pltpu.VMEM((18, 10, 32, 1024), BF),
            pltpu.VMEM((10, 16, 1024), BF),
            pltpu.VMEM((1024, 1024), BF),
            pltpu.VMEM((2, 1024, 128), F32),
            pltpu.VMEM((2, 16, 256), BF),
            pltpu.VMEM((2, 256, 256), BF),
            pltpu.VMEM((2, 3, 16, 256), BF),
            pltpu.VMEM((2, 48, 1024), F32),
            pltpu.VMEM((48, 256), F32),
            pltpu.VMEM((512, 128), F32),
            pltpu.VMEM((2, 64, 512), F32),
            units,
            units,
            pltpu.VMEM((2, 1024, 128), F32),
            pltpu.VMEM((2, 1024, 128), F32),
            units,
            units,
            pltpu.VMEM((4, 8, 128, 256), BF),
            pltpu.SemaphoreType.DMA((8,)),
            pltpu.SemaphoreType.DMA((8,)),
            pltpu.SemaphoreType.DMA((4,)),
            pltpu.SemaphoreType.DMA((4,)),
            pltpu.SemaphoreType.DMA((4,)),
            pltpu.SemaphoreType.DMA((4,)),
            pltpu.SemaphoreType.DMA((4,)),
            pltpu.SemaphoreType.DMA((7,)),
        ],
        compiler_params=pltpu.CompilerParams(
            collective_id=0, has_side_effects=True, vmem_limit_bytes=60 * 1024 * 1024
        ),
        cost_estimate=pl.CostEstimate(
            flops=20_000_000_000, bytes_accessed=8_000_000, transcendentals=20_000_000
        ),
        name="maxvit",
    )(
        tokens,
        bn_scale.reshape(1, -1),
        bn_shift.reshape(1, -1),
        w_expand,
        b_expand.reshape(1, -1),
        dw_kernel,
        dw_bias.reshape(1, -1),
        w_project,
        b_project.reshape(1, -1),
        norm_gains,
        attn_qkv,
        attn_out,
        rel_bias.reshape(16, 225),
        mlp_up,
        mlp_down,
    )


def solution(mesh):
    placed = (P("row", "col", None),) + (P(),) * 14
    return jax.shard_map(
        on_device, mesh=mesh, in_specs=placed, out_specs=P("row", "col", None), check_vma=False
    )
```

```python
import math

import jax
import jax.numpy as jnp
from jax import lax
from jax.experimental import pallas as pl
from jax.experimental.pallas import tpu as pltpu
from jax.sharding import PartitionSpec as P

WIN = 8
BF = jnp.bfloat16
F32 = jnp.float32
MESH = pl.DeviceIdType.MESH


def gelu_of_half(h):
    h = h.astype(BF)
    inner = h * (BF(2 * 0.7978845608) + BF(8 * 0.0356774081) * (h * h))
    return h + h * jnp.tanh(inner)


def dot(a, b):
    return jnp.dot(a, b, preferred_element_type=F32)


def layer_norm(x, gain):
    center = x - jnp.mean(x, axis=-1, keepdims=True)
    spread = jnp.mean(center * center, axis=-1, keepdims=True)
    return (center * lax.rsqrt(spread + 1e-05) * gain).astype(BF)


def attend(x, gain, w_qkv, w_out, bias, head_masks):
    qkv = dot(layer_norm(x, gain), w_qkv[...])
    q = (qkv[:, :256] * (math.log2(math.e) / math.sqrt(32.0))).astype(BF)
    k = qkv[:, 256:512].astype(BF)
    v = qkv[:, 512:].astype(BF)
    low = lax.broadcasted_iota(jnp.int32, (64, 128), 1) < 64
    n_windows = x.shape[0] // 64
    pairs = [(w, g) for w in range(n_windows) for g in range(2)]

    def scores(w, g):
        rows, lanes = slice(64 * w, 64 * w + 64), slice(128 * g, 128 * g + 128)
        kk = k[rows, lanes]
        k_diag = jnp.concatenate([kk * m for m in head_masks], axis=0)
        return lax.dot_general(
            q[rows, lanes], k_diag, (((1,), (1,)), ((), ())), preferred_element_type=F32
        )

    def probabilities(s, g):
        s = s + bias[:, 256 * g : 256 * g + 256]
        probs = []
        for p in range(2):
            sp = s[:, 128 * p : 128 * p + 128]
            top_lo = jnp.max(jnp.where(low, sp, -jnp.inf), axis=-1, keepdims=True)
            top_hi = jnp.max(jnp.where(low, -jnp.inf, sp), axis=-1, keepdims=True)
            probs.append(jnp.exp2(sp - jnp.where(low, top_lo, top_hi)).astype(BF))
        return jnp.concatenate(probs, axis=1)

    def context(p4, w, g):
        vv = v[64 * w : 64 * w + 64, 128 * g : 128 * g + 128]
        v_diag = jnp.concatenate([jnp.concatenate([vv * m, m], axis=1) for m in head_masks], axis=0)
        o = dot(p4, v_diag)
        return (o[:, :128] / o[:, 128:]).astype(BF)

    found = [scores(w, g) for w, g in pairs]
    found = [probabilities(s, g) for s, (w, g) in zip(found, pairs)]
    halves = [context(p4, w, g) for p4, (w, g) in zip(found, pairs)]
    contexts = [
        jnp.concatenate(halves[2 * w : 2 * w + 2], axis=1) for w in range(n_windows)
    ]
    return x + dot(jnp.concatenate(contexts, axis=0), w_out[...])


def mlp(y, gain, w_up, w_down):
    h = gelu_of_half(dot(layer_norm(y, gain * 0.5), w_up[...]))
    return y + dot(h, w_down[...])


def fill_bias(rel_bias, split, looked_up, bias):
    rest = rel_bias[...] * math.log2(math.e)
    split[...] = jnp.zeros_like(split)
    for n in range(3):
        piece = rest.astype(BF)
        rest = rest - piece.astype(F32)
        split[16 * n : 16 * n + 16, :225] = piece.astype(F32)
    lane = lax.broadcasted_iota(jnp.int32, (1, 4096), 1)
    q = lax.rem(lane // 64, 2) * 32 + lane // 128
    k = lax.rem(lane, 64)
    entry = (q // 8 - k // 8 + 7) * 15 + lax.rem(q, 8) - lax.rem(k, 8) + 7
    onehot = jnp.where(lax.broadcasted_iota(jnp.int32, (256, 4096), 0) == entry, 1.0, 0.0)
    found = dot(split[...].astype(BF), onehot.astype(BF))
    found = found[:16] + found[16:32] + found[32:]
    for t in range(32):
        looked_up[16 * t : 16 * t + 16, :] = found[:, 128 * t : 128 * t + 128]
    low = lax.broadcasted_iota(jnp.int32, (32, 128), 1) < 64
    for i in range(2):
        for pair in range(4):
            even = looked_up[pl.ds(8 * i + 2 * pair, 32, stride=16), :]
            odd = looked_up[pl.ds(8 * i + 2 * pair + 1, 32, stride=16), :]
            lanes = slice(128 * pair, 128 * pair + 128)
            bias[i, :32, lanes] = jnp.where(low, even, pltpu.roll(odd, 64, 1))
            bias[i, 32:, lanes] = jnp.where(low, pltpu.roll(even, 64, 1), odd)


def body(
    tokens_hbm,
    bn_scale,
    bn_shift,
    w_expand_hbm,
    b_expand,
    dw_kernel,
    dw_bias,
    w_project_hbm,
    b_project,
    gains,
    w_qkv_hbm,
    w_out_hbm,
    rel_bias,
    w_up_hbm,
    w_down_hbm,
    out,
    tokens,
    w_expand,
    w_project,
    w_qkv,
    w_out,
    w_up,
    w_down,
    xf,
    hid,
    taps,
    act,
    conv,
    edge,
    halo_row,
    halo_col,
    halo_hid,
    split,
    looked_up,
    bias,
    send,
    recv,
    gathered,
    finished,
    ret,
    back,
    done,
    halo_send_sem,
    halo_recv_sem,
    go_send_sem,
    go_recv_sem,
    back_send_sem,
    back_recv_sem,
    out_sem,
    load_sem,
):
    row = lax.axis_index("row")
    col = lax.axis_index("col")
    core = lax.rem(row, 2)
    pa = row // 2
    me = pa * 8 + col

    def device(index):
        return (2 * (index // 8) + core, lax.rem(index, 8))

    loads = [
        pltpu.make_async_copy(source, target, load_sem.at[n])
        for n, (source, target) in enumerate(
            (
                (tokens_hbm, tokens),
                (w_expand_hbm, w_expand),
                (w_project_hbm, w_project),
                (w_qkv_hbm, w_qkv),
                (w_out_hbm, w_out),
                (w_up_hbm, w_up),
                (w_down_hbm, w_down),
            )
        )
    ]
    for load in loads:
        load.start()

    barrier = pltpu.get_barrier_semaphore()

    @pl.loop(1, 64)
    def _(step):
        pl.semaphore_signal(
            barrier, inc=1, device_id=device(lax.rem(me + step, 64)), device_id_type=MESH
        )

    up, down = lax.rem(row + 15, 16), lax.rem(row + 1, 16)
    left, right = lax.rem(col + 7, 8), lax.rem(col + 1, 8)
    for r in (up, down):
        for c in (left, col, right):
            pl.semaphore_signal(barrier, inc=1, device_id=(r, c), device_id_type=MESH)

    def load_rows(source, at):
        for half in range(2):
            xf[half, pl.ds(pl.multiple_of(at * 256, 256), 256), :] = source[
                :, 128 * half : 128 * half + 128
            ].astype(F32)

    loads[0].wait()

    @pl.loop(0, 16)
    def _(r):
        load_rows(tokens[r], r)

    for side in range(2):
        column = [xf[half, pl.ds(255 * side, 16, stride=256), :] for half in range(2)]
        edge[side] = jnp.concatenate(column, axis=1).astype(BF)
    for t in range(9):
        tap = dw_kernel[t // 3, t % 3 : t % 3 + 1, :]
        taps[t] = jnp.broadcast_to(tap * 0.5, (16, 1024)).astype(BF)
    taps[9] = jnp.broadcast_to(dw_bias[...] * 0.5, (16, 1024)).astype(BF)

    pl.semaphore_wait(barrier, 69)

    halo_copies = []

    def send_halo(src, dst, to):
        n = len(halo_copies)
        copy = pltpu.make_async_remote_copy(
            src_ref=src,
            dst_ref=dst,
            send_sem=halo_send_sem.at[n],
            recv_sem=halo_recv_sem.at[n],
            device_id=to,
            device_id_type=MESH,
        )
        copy.start()
        halo_copies.append(copy)

    send_halo(tokens.at[0], halo_row.at[1], (up, col))
    send_halo(tokens.at[15], halo_row.at[0], (down, col))
    for r, slot in ((up, 2), (row, 1), (down, 0)):
        send_halo(edge.at[0], halo_col.at[1, slot], (r, left))
        send_halo(edge.at[1], halo_col.at[0, slot], (r, right))

    def normed_half(x):
        return (x * (bn_scale[...] * 0.5) + bn_shift[...] * 0.5).astype(BF)

    def expand(normed, lanes):
        return gelu_of_half(dot(normed, w_expand[:, lanes]) + b_expand[:, lanes] * 0.5)

    def hidden_rows(source, at, masks):
        count = len(masks)
        x = [
            jnp.concatenate(
                [xf[half, pl.ds((source + i) * 256 + j, 32, stride=8), :] for half in range(2)],
                axis=1,
            )
            for i in range(count)
            for j in range(8)
        ]
        normed = normed_half(jnp.concatenate(x, axis=0))
        for n in range(4):
            lanes = slice(256 * n, 256 * n + 256)
            rows = expand(normed, lanes)
            for i, mask in enumerate(masks):
                h = rows[256 * i : 256 * i + 256]
                if mask is not None:
                    h = h * mask
                hid[at + i, 1:9, :, lanes] = h.reshape(8, 32, 256)
                first, last = h[:32].astype(F32), h[224:].astype(F32)
                hid[at + i, 0, :, lanes] = pltpu.roll(last, 1, 0).astype(BF)
                hid[at + i, 9, :, lanes] = pltpu.roll(first, 31, 0).astype(BF)

    top = jnp.where(row > 0, 1.0, 0.0).astype(F32)
    bottom = jnp.where(row < 15, 1.0, 0.0).astype(F32)
    place = lax.broadcasted_iota(jnp.int32, (16, 1024), 0)

    def place_edges(r):
        for side in range(2):
            beside = halo_hid[side, 15 + r : 16 + r, :]
            if r in (0, 17):
                beside = beside * (top if r == 0 else bottom)
            rows = slice(16 * side, 16 * side + 16)
            old = hid[r, 9 * side, rows].astype(F32)
            hid[r, 9 * side, rows] = jnp.where(place == 15 * side, beside, old).astype(BF)

    fill_bias(rel_bias, split, looked_up, bias)
    loads[1].wait()

    @pl.loop(0, 5)
    def _(r):
        hidden_rows(r * 3, r * 3 + 1, [None] * 3)

    for copy in halo_copies:
        copy.wait()

    load_rows(halo_row[1], 16)
    load_rows(halo_row[0], 17)
    hidden_rows(17, 0, [top.astype(BF)])
    for side, inside in ((0, col > 0), (1, col < 7)):
        x = halo_col[side].reshape(48, 256).astype(F32)
        h = expand(normed_half(x), slice(0, 1024)).astype(F32)
        halo_hid[side] = h * jnp.where(inside, 1.0, 0.0).astype(F32)
    for r in range(10):
        place_edges(r)

    lane = lax.broadcasted_iota(jnp.int32, (64, 128), 1) // 32
    head_masks = [jnp.where(lane == h, 1.0, 0.0).astype(BF) for h in range(4)]

    x_chip, y_chip, z_chip = (col // 4) * 2 + lax.rem(pa, 2), pa // 2, lax.rem(col, 4)

    to_x = [lax.rem(x_chip + d, 4) for d in range(4)]
    to_y = [lax.rem(y_chip + d, 4) for d in range(4)]
    to_z = [lax.rem(z_chip + d, 4) for d in range(4)]
    offsets = sorted(
        ((y, x, z) for y in range(4) for x in range(4) for z in range(4)),
        key=lambda o: (-sum(min(d, 4 - d) for d in o), (o[0] + o[1] + 2 * o[2]) % 4, o),
    )[:-1]

    def push_units(part, source, target, send_sem, recv_sem):
        for y, x, z in offsets:
            to_pa = to_y[y] * 2 + lax.rem(to_x[x], 2)
            to_col = (to_x[x] // 2) * 4 + to_z[z]
            pltpu.make_async_remote_copy(
                src_ref=source.at[part, to_pa * 8 + to_col],
                dst_ref=target.at[part, me],
                send_sem=send_sem.at[part],
                recv_sem=recv_sem.at[part],
                device_id=(2 * to_pa + core, to_col),
                device_id_type=MESH,
            ).start()

    def conv_part(band, side):
        columns = pl.ds(pl.multiple_of(side * 16, 16), 16)

        @pl.loop(0, 4)
        def _(pair):
            for n in range(8):
                lanes = slice(128 * n, 128 * n + 128)
                weights = [taps[t, :, lanes] for t in range(10)]
                window = [
                    [hid[band * 8 + pair * 2 + a, j, columns, lanes] for a in range(4)]
                    for j in range(10)
                ]
                results = []
                for j in range(8):
                    for i in range(2):
                        total = weights[9]
                        for b in range(3):
                            for a in range(3):
                                total = total + window[j + b][i + a] * weights[3 * a + b]
                        results.append(gelu_of_half(total))
                for j in range(8):
                    for i in range(2):
                        at = pl.multiple_of(pair * 256 + i * 128 + j * 16, 16)
                        act[pl.ds(at, 16), lanes] = results[2 * j + i]

        x = [
            jnp.concatenate(
                [
                    xf[half, pl.ds((band * 8 + r) * 256 + side * 128 + j, 16, stride=8), :]
                    for half in range(2)
                ],
                axis=1,
            )
            for r in range(8)
            for j in range(8)
        ]
        y = jnp.concatenate(x, axis=0) + dot(act[...], w_project[...]) + b_project[...]
        for half in range(2):
            conv[half, :, :] = y[:, 128 * half : 128 * half + 128]

    def block_part(part):
        pieces = [
            jnp.concatenate(
                [conv[half, pl.ds(r * 128 + s, 8, stride=16), :] for half in range(2)], axis=1
            )
            for s in range(16)
            for r in range(8)
        ]
        y = attend(
            jnp.concatenate(pieces, axis=0),
            gains[0:1, :],
            w_qkv.at[0],
            w_out.at[0],
            bias.at[0],
            head_masks,
        )
        y = mlp(y, gains[1:2, :], w_up.at[0], w_down.at[0])
        for s in range(8):
            for r in range(8):
                at = 128 * s + 8 * r
                unit = jnp.concatenate([y[at : at + 8], y[at + 64 : at + 72]], axis=0)
                send[part, r * 8 + s] = unit.astype(BF)

        push_units(part, send, recv, go_send_sem, go_recv_sem)

        recv[part, me] = send[part, me]

    def grid_part(part):
        others = recv.at[part, pl.ds(0, 63)]
        pltpu.make_async_copy(others, others, go_recv_sem.at[part]).wait()

        @pl.loop(0, 4)
        def _(piece):
            block = recv[part, pl.ds(piece * 16, 16)].reshape(256, 256)
            for half in range(2):
                gathered[half, pl.ds(pl.multiple_of(piece * 256, 256), 256), :] = block[
                    :, 128 * half : 128 * half + 128
                ].astype(F32)

        windows = [
            jnp.concatenate([gathered[half, pl.ds(t, 64, stride=16), :] for half in range(2)], axis=1)
            for t in range(16)
        ]
        y = attend(
            jnp.concatenate(windows, axis=0),
            gains[2:3, :],
            w_qkv.at[1],
            w_out.at[1],
            bias.at[1],
            head_masks,
        )
        for half in range(2):
            finished[half, :, :] = y[:, 128 * half : 128 * half + 128]
        for source in range(64):
            unit = [finished[half, pl.ds(source, 16, stride=64), :] for half in range(2)]
            ret[part, source] = jnp.concatenate(unit, axis=1).astype(BF)

        push_units(part, ret, back, back_send_sem, back_recv_sem)

        back[part, me] = ret[part, me]

    for load in loads[2:]:
        load.wait()

    @pl.loop(0, 6)
    def _(step):
        @pl.when(step == 2)
        def _():
            hidden_rows(15, 16, [None, bottom.astype(BF)])
            for r in range(10, 18):
                place_edges(r)

        @pl.when(step < 4)
        def _():
            conv_part(step // 2, lax.rem(step, 2))
            block_part(step)

        @pl.when(step >= 2)
        def _():
            grid_part(step - 2)

    def store(part):
        return pltpu.make_async_copy(
            done.at[part],
            out.at[
                pl.ds((part // 2) * 8, 8), pl.ds(pl.multiple_of(lax.rem(part, 2) * 128, 128), 128)
            ],
            out_sem.at[part],
        )

    @pl.loop(0, 4)
    def _(part):
        others = back.at[part, pl.ds(0, 63)]
        pltpu.make_async_copy(others, others, back_recv_sem.at[part]).wait()
        y = back[part].reshape(1024, 256).astype(F32)
        y = mlp(y, gains[3:4, :], w_up.at[1], w_down.at[1])
        done[part] = y.astype(BF).reshape(8, 128, 256)
        store(part).start()

    @pl.loop(0, 4)
    def _(part):
        sent = send.at[part, pl.ds(0, 63)]
        pltpu.make_async_copy(sent, sent, go_send_sem.at[part]).wait()
        returned = ret.at[part, pl.ds(0, 63)]
        pltpu.make_async_copy(returned, returned, back_send_sem.at[part]).wait()
        store(part).wait()


def on_device(
    tokens,
    bn_scale,
    bn_shift,
    w_expand,
    b_expand,
    dw_kernel,
    dw_bias,
    w_project,
    b_project,
    norm_gains,
    attn_qkv,
    attn_out,
    rel_bias,
    mlp_up,
    mlp_down,
):
    vmem = pl.BlockSpec(memory_space=pltpu.VMEM)
    hbm = pl.BlockSpec(memory_space=pl.ANY)
    units = pltpu.VMEM((4, 64, 16, 256), BF)
    return pl.pallas_call(
        body,
        out_shape=jax.ShapeDtypeStruct((16, 256, 256), BF),
        in_specs=[hbm, vmem, vmem, hbm, vmem, vmem, vmem, hbm, vmem, vmem, hbm, hbm, vmem, hbm, hbm],
        out_specs=pl.BlockSpec(memory_space=pl.ANY),
        scratch_shapes=[
            pltpu.VMEM((16, 256, 256), BF),
            pltpu.VMEM((256, 1024), BF),
            pltpu.VMEM((1024, 256), BF),
            pltpu.VMEM((2, 256, 768), BF),
            pltpu.VMEM((2, 256, 256), BF),
            pltpu.VMEM((2, 256, 1024), BF),
            pltpu.VMEM((2, 1024, 256), BF),
            pltpu.VMEM((2, 18 * 256, 128), F32),
            pltpu.VMEM((18, 10, 32, 1024), BF),
            pltpu.VMEM((10, 16, 1024), BF),
            pltpu.VMEM((1024, 1024), BF),
            pltpu.VMEM((2, 1024, 128), F32),
            pltpu.VMEM((2, 16, 256), BF),
            pltpu.VMEM((2, 256, 256), BF),
            pltpu.VMEM((2, 3, 16, 256), BF),
            pltpu.VMEM((2, 48, 1024), F32),
            pltpu.VMEM((48, 256), F32),
            pltpu.VMEM((512, 128), F32),
            pltpu.VMEM((2, 64, 512), F32),
            units,
            units,
            pltpu.VMEM((2, 1024, 128), F32),
            pltpu.VMEM((2, 1024, 128), F32),
            units,
            units,
            pltpu.VMEM((4, 8, 128, 256), BF),
            pltpu.SemaphoreType.DMA((8,)),
            pltpu.SemaphoreType.DMA((8,)),
            pltpu.SemaphoreType.DMA((4,)),
            pltpu.SemaphoreType.DMA((4,)),
            pltpu.SemaphoreType.DMA((4,)),
            pltpu.SemaphoreType.DMA((4,)),
            pltpu.SemaphoreType.DMA((4,)),
            pltpu.SemaphoreType.DMA((7,)),
        ],
        compiler_params=pltpu.CompilerParams(
            collective_id=0, has_side_effects=True, vmem_limit_bytes=60 * 1024 * 1024
        ),
        cost_estimate=pl.CostEstimate(
            flops=20_000_000_000, bytes_accessed=8_000_000, transcendentals=20_000_000
        ),
        name="maxvit",
    )(
        tokens,
        bn_scale.reshape(1, -1),
        bn_shift.reshape(1, -1),
        w_expand,
        b_expand.reshape(1, -1),
        dw_kernel,
        dw_bias.reshape(1, -1),
        w_project,
        b_project.reshape(1, -1),
        norm_gains,
        attn_qkv,
        attn_out,
        rel_bias.reshape(16, 225),
        mlp_up,
        mlp_down,
    )


def solution(mesh):
    placed = (P("row", "col", None),) + (P(),) * 14
    return jax.shard_map(
        on_device, mesh=mesh, in_specs=placed, out_specs=P("row", "col", None), check_vma=False
    )
```

```python
import math

import jax
import jax.numpy as jnp
from jax import lax
from jax.experimental import pallas as pl
from jax.experimental.pallas import tpu as pltpu
from jax.sharding import PartitionSpec as P

WIN = 8
BF = jnp.bfloat16
F32 = jnp.float32
MESH = pl.DeviceIdType.MESH


def gelu_of_half(h):
    h = h.astype(BF)
    inner = h * (BF(2 * 0.7978845608) + BF(8 * 0.0356774081) * (h * h))
    return h + h * jnp.tanh(inner)


def dot(a, b):
    return jnp.dot(a, b, preferred_element_type=F32)


def layer_norm(x, gain):
    center = x - jnp.mean(x, axis=-1, keepdims=True)
    spread = jnp.mean(center * center, axis=-1, keepdims=True)
    return (center * lax.rsqrt(spread + 1e-05) * gain).astype(BF)


def attend(x, gain, w_qkv, w_out, bias, head_masks):
    qkv = dot(layer_norm(x, gain), w_qkv[...])
    q = (qkv[:, :256] * (math.log2(math.e) / math.sqrt(32.0))).astype(BF)
    k = qkv[:, 256:512].astype(BF)
    v = qkv[:, 512:].astype(BF)
    low = lax.broadcasted_iota(jnp.int32, (64, 128), 1) < 64
    n_windows = x.shape[0] // 64
    pairs = [(w, g) for w in range(n_windows) for g in range(2)]

    def scores(w, g):
        rows, lanes = slice(64 * w, 64 * w + 64), slice(128 * g, 128 * g + 128)
        kk = k[rows, lanes]
        k_diag = jnp.concatenate([kk * m for m in head_masks], axis=0)
        return lax.dot_general(
            q[rows, lanes], k_diag, (((1,), (1,)), ((), ())), preferred_element_type=F32
        )

    def probabilities(s, g):
        s = s + bias[:, 256 * g : 256 * g + 256]
        probs = []
        for p in range(2):
            sp = s[:, 128 * p : 128 * p + 128]
            top_lo = jnp.max(jnp.where(low, sp, -jnp.inf), axis=-1, keepdims=True)
            top_hi = jnp.max(jnp.where(low, -jnp.inf, sp), axis=-1, keepdims=True)
            probs.append(jnp.exp2(sp - jnp.where(low, top_lo, top_hi)).astype(BF))
        return jnp.concatenate(probs, axis=1)

    def context(p4, w, g):
        vv = v[64 * w : 64 * w + 64, 128 * g : 128 * g + 128]
        v_diag = jnp.concatenate([jnp.concatenate([vv * m, m], axis=1) for m in head_masks], axis=0)
        o = dot(p4, v_diag)
        return (o[:, :128] / o[:, 128:]).astype(BF)

    found = [scores(w, g) for w, g in pairs]
    found = [probabilities(s, g) for s, (w, g) in zip(found, pairs)]
    halves = [context(p4, w, g) for p4, (w, g) in zip(found, pairs)]
    contexts = [
        jnp.concatenate(halves[2 * w : 2 * w + 2], axis=1) for w in range(n_windows)
    ]
    return x + dot(jnp.concatenate(contexts, axis=0), w_out[...])


def mlp(y, gain, w_up, w_down):
    h = gelu_of_half(dot(layer_norm(y, gain * 0.5), w_up[...]))
    return y + dot(h, w_down[...])


def fill_bias(rel_bias, split, looked_up, bias):
    rest = rel_bias[...] * math.log2(math.e)
    split[...] = jnp.zeros_like(split)
    for n in range(3):
        piece = rest.astype(BF)
        rest = rest - piece.astype(F32)
        split[16 * n : 16 * n + 16, :225] = piece.astype(F32)
    lane = lax.broadcasted_iota(jnp.int32, (1, 4096), 1)
    q = lax.rem(lane // 64, 2) * 32 + lane // 128
    k = lax.rem(lane, 64)
    entry = (q // 8 - k // 8 + 7) * 15 + lax.rem(q, 8) - lax.rem(k, 8) + 7
    onehot = jnp.where(lax.broadcasted_iota(jnp.int32, (256, 4096), 0) == entry, 1.0, 0.0)
    found = dot(split[...].astype(BF), onehot.astype(BF))
    found = found[:16] + found[16:32] + found[32:]
    for t in range(32):
        looked_up[16 * t : 16 * t + 16, :] = found[:, 128 * t : 128 * t + 128]
    low = lax.broadcasted_iota(jnp.int32, (32, 128), 1) < 64
    for i in range(2):
        for pair in range(4):
            even = looked_up[pl.ds(8 * i + 2 * pair, 32, stride=16), :]
            odd = looked_up[pl.ds(8 * i + 2 * pair + 1, 32, stride=16), :]
            lanes = slice(128 * pair, 128 * pair + 128)
            bias[i, :32, lanes] = jnp.where(low, even, pltpu.roll(odd, 64, 1))
            bias[i, 32:, lanes] = jnp.where(low, pltpu.roll(even, 64, 1), odd)


def body(
    tokens_hbm,
    bn_scale,
    bn_shift,
    w_expand_hbm,
    b_expand,
    dw_kernel,
    dw_bias,
    w_project_hbm,
    b_project,
    gains,
    w_qkv_hbm,
    w_out_hbm,
    rel_bias,
    w_up_hbm,
    w_down_hbm,
    out,
    tokens,
    w_expand,
    w_project,
    w_qkv,
    w_out,
    w_up,
    w_down,
    xf,
    hid,
    taps,
    act,
    conv,
    edge,
    halo_row,
    halo_col,
    halo_hid,
    split,
    looked_up,
    bias,
    send,
    recv,
    gathered,
    finished,
    ret,
    back,
    done,
    halo_send_sem,
    halo_recv_sem,
    go_send_sem,
    go_recv_sem,
    back_send_sem,
    back_recv_sem,
    out_sem,
    load_sem,
):
    row = lax.axis_index("row")
    col = lax.axis_index("col")
    core = lax.rem(row, 2)
    pa = row // 2
    me = pa * 8 + col

    def device(index):
        return (2 * (index // 8) + core, lax.rem(index, 8))

    loads = [
        pltpu.make_async_copy(source, target, load_sem.at[n])
        for n, (source, target) in enumerate(
            (
                (tokens_hbm, tokens),
                (w_expand_hbm, w_expand),
                (w_project_hbm, w_project),
                (w_qkv_hbm, w_qkv),
                (w_out_hbm, w_out),
                (w_up_hbm, w_up),
                (w_down_hbm, w_down),
            )
        )
    ]
    for load in loads:
        load.start()

    barrier = pltpu.get_barrier_semaphore()

    @pl.loop(1, 64)
    def _(step):
        pl.semaphore_signal(
            barrier, inc=1, device_id=device(lax.rem(me + step, 64)), device_id_type=MESH
        )

    up, down = lax.rem(row + 15, 16), lax.rem(row + 1, 16)
    left, right = lax.rem(col + 7, 8), lax.rem(col + 1, 8)
    for r in (up, down):
        for c in (left, col, right):
            pl.semaphore_signal(barrier, inc=1, device_id=(r, c), device_id_type=MESH)

    def load_rows(source, at):
        for half in range(2):
            xf[half, pl.ds(pl.multiple_of(at * 256, 256), 256), :] = source[
                :, 128 * half : 128 * half + 128
            ].astype(F32)

    loads[0].wait()

    @pl.loop(0, 16, unroll=4)
    def _(r):
        load_rows(tokens[r], r)

    for side in range(2):
        column = [xf[half, pl.ds(255 * side, 16, stride=256), :] for half in range(2)]
        edge[side] = jnp.concatenate(column, axis=1).astype(BF)
    for t in range(9):
        tap = dw_kernel[t // 3, t % 3 : t % 3 + 1, :]
        taps[t] = jnp.broadcast_to(tap * 0.5, (16, 1024)).astype(BF)
    taps[9] = jnp.broadcast_to(dw_bias[...] * 0.5, (16, 1024)).astype(BF)

    fill_bias(rel_bias, split, looked_up, bias)

    pl.semaphore_wait(barrier, 69)

    halo_copies = []

    def send_halo(src, dst, to):
        n = len(halo_copies)
        copy = pltpu.make_async_remote_copy(
            src_ref=src,
            dst_ref=dst,
            send_sem=halo_send_sem.at[n],
            recv_sem=halo_recv_sem.at[n],
            device_id=to,
            device_id_type=MESH,
        )
        copy.start()
        halo_copies.append(copy)

    send_halo(tokens.at[0], halo_row.at[1], (up, col))
    send_halo(tokens.at[15], halo_row.at[0], (down, col))
    for r, slot in ((up, 2), (row, 1), (down, 0)):
        send_halo(edge.at[0], halo_col.at[1, slot], (r, left))
        send_halo(edge.at[1], halo_col.at[0, slot], (r, right))

    def normed_half(x):
        return (x * (bn_scale[...] * 0.5) + bn_shift[...] * 0.5).astype(BF)

    def expand(normed, lanes):
        return gelu_of_half(dot(normed, w_expand[:, lanes]) + b_expand[:, lanes] * 0.5)

    def hidden_rows(source, at, masks):
        count = len(masks)
        x = [
            jnp.concatenate(
                [xf[half, pl.ds((source + i) * 256 + j, 32, stride=8), :] for half in range(2)],
                axis=1,
            )
            for i in range(count)
            for j in range(8)
        ]
        normed = normed_half(jnp.concatenate(x, axis=0))
        for n in range(4):
            lanes = slice(256 * n, 256 * n + 256)
            rows = expand(normed, lanes)
            for i, mask in enumerate(masks):
                h = rows[256 * i : 256 * i + 256]
                if mask is not None:
                    h = h * mask
                hid[at + i, 1:9, :, lanes] = h.reshape(8, 32, 256)
                first, last = h[:32].astype(F32), h[224:].astype(F32)
                hid[at + i, 0, :, lanes] = pltpu.roll(last, 1, 0).astype(BF)
                hid[at + i, 9, :, lanes] = pltpu.roll(first, 31, 0).astype(BF)

    top = jnp.where(row > 0, 1.0, 0.0).astype(F32)
    bottom = jnp.where(row < 15, 1.0, 0.0).astype(F32)
    place = lax.broadcasted_iota(jnp.int32, (16, 1024), 0)

    def place_edges(r):
        for side in range(2):
            beside = halo_hid[side, 15 + r : 16 + r, :]
            if r in (0, 17):
                beside = beside * (top if r == 0 else bottom)
            rows = slice(16 * side, 16 * side + 16)
            old = hid[r, 9 * side, rows].astype(F32)
            hid[r, 9 * side, rows] = jnp.where(place == 15 * side, beside, old).astype(BF)

    loads[1].wait()

    @pl.loop(0, 5)
    def _(r):
        hidden_rows(r * 3, r * 3 + 1, [None] * 3)

    for copy in halo_copies:
        copy.wait()

    load_rows(halo_row[1], 16)
    load_rows(halo_row[0], 17)
    hidden_rows(17, 0, [top.astype(BF)])
    for side, inside in ((0, col > 0), (1, col < 7)):
        x = halo_col[side].reshape(48, 256).astype(F32)
        h = expand(normed_half(x), slice(0, 1024)).astype(F32)
        halo_hid[side] = h * jnp.where(inside, 1.0, 0.0).astype(F32)
    for r in range(10):
        place_edges(r)

    lane = lax.broadcasted_iota(jnp.int32, (64, 128), 1) // 32
    head_masks = [jnp.where(lane == h, 1.0, 0.0).astype(BF) for h in range(4)]

    x_chip, y_chip, z_chip = (col // 4) * 2 + lax.rem(pa, 2), pa // 2, lax.rem(col, 4)

    to_x = [lax.rem(x_chip + d, 4) for d in range(4)]
    to_y = [lax.rem(y_chip + d, 4) for d in range(4)]
    to_z = [lax.rem(z_chip + d, 4) for d in range(4)]
    offsets = sorted(
        ((y, x, z) for y in range(4) for x in range(4) for z in range(4)),
        key=lambda o: (-sum(min(d, 4 - d) for d in o), (o[0] + o[1] + 2 * o[2]) % 4, o),
    )[:-1]

    def push_units(part, source, target, send_sem, recv_sem):
        for y, x, z in offsets:
            to_pa = to_y[y] * 2 + lax.rem(to_x[x], 2)
            to_col = (to_x[x] // 2) * 4 + to_z[z]
            pltpu.make_async_remote_copy(
                src_ref=source.at[part, to_pa * 8 + to_col],
                dst_ref=target.at[part, me],
                send_sem=send_sem.at[part],
                recv_sem=recv_sem.at[part],
                device_id=(2 * to_pa + core, to_col),
                device_id_type=MESH,
            ).start()

    def conv_part(band, side):
        columns = pl.ds(pl.multiple_of(side * 16, 16), 16)

        @pl.loop(0, 4)
        def _(pair):
            for n in range(8):
                lanes = slice(128 * n, 128 * n + 128)
                weights = [taps[t, :, lanes] for t in range(10)]
                window = [
                    [hid[band * 8 + pair * 2 + a, j, columns, lanes] for a in range(4)]
                    for j in range(10)
                ]
                results = []
                for j in range(8):
                    for i in range(2):
                        total = weights[9]
                        for b in range(3):
                            for a in range(3):
                                total = total + window[j + b][i + a] * weights[3 * a + b]
                        results.append(gelu_of_half(total))
                for j in range(8):
                    for i in range(2):
                        at = pl.multiple_of(pair * 256 + i * 128 + j * 16, 16)
                        act[pl.ds(at, 16), lanes] = results[2 * j + i]

        x = [
            jnp.concatenate(
                [
                    xf[half, pl.ds((band * 8 + r) * 256 + side * 128 + j, 16, stride=8), :]
                    for half in range(2)
                ],
                axis=1,
            )
            for r in range(8)
            for j in range(8)
        ]
        y = jnp.concatenate(x, axis=0) + dot(act[...], w_project[...]) + b_project[...]
        for half in range(2):
            conv[half, :, :] = y[:, 128 * half : 128 * half + 128]

    def block_part(part):
        pieces = [
            jnp.concatenate(
                [conv[half, pl.ds(r * 128 + s, 8, stride=16), :] for half in range(2)], axis=1
            )
            for s in range(16)
            for r in range(8)
        ]
        y = attend(
            jnp.concatenate(pieces, axis=0),
            gains[0:1, :],
            w_qkv.at[0],
            w_out.at[0],
            bias.at[0],
            head_masks,
        )
        y = mlp(y, gains[1:2, :], w_up.at[0], w_down.at[0])
        for s in range(8):
            for r in range(8):
                at = 128 * s + 8 * r
                unit = jnp.concatenate([y[at : at + 8], y[at + 64 : at + 72]], axis=0)
                send[part, r * 8 + s] = unit.astype(BF)

        push_units(part, send, recv, go_send_sem, go_recv_sem)

        recv[part, me] = send[part, me]

    def grid_part(part):
        others = recv.at[part, pl.ds(0, 63)]
        pltpu.make_async_copy(others, others, go_recv_sem.at[part]).wait()

        @pl.loop(0, 4)
        def _(piece):
            block = recv[part, pl.ds(piece * 16, 16)].reshape(256, 256)
            for half in range(2):
                gathered[half, pl.ds(pl.multiple_of(piece * 256, 256), 256), :] = block[
                    :, 128 * half : 128 * half + 128
                ].astype(F32)

        windows = [
            jnp.concatenate([gathered[half, pl.ds(t, 64, stride=16), :] for half in range(2)], axis=1)
            for t in range(16)
        ]
        y = attend(
            jnp.concatenate(windows, axis=0),
            gains[2:3, :],
            w_qkv.at[1],
            w_out.at[1],
            bias.at[1],
            head_masks,
        )
        for half in range(2):
            finished[half, :, :] = y[:, 128 * half : 128 * half + 128]
        for source in range(64):
            unit = [finished[half, pl.ds(source, 16, stride=64), :] for half in range(2)]
            ret[part, source] = jnp.concatenate(unit, axis=1).astype(BF)

        push_units(part, ret, back, back_send_sem, back_recv_sem)

        back[part, me] = ret[part, me]

    for load in loads[2:]:
        load.wait()

    @pl.loop(0, 6)
    def _(step):
        @pl.when(step == 2)
        def _():
            hidden_rows(15, 16, [None, bottom.astype(BF)])
            for r in range(10, 18):
                place_edges(r)

        @pl.when(step < 4)
        def _():
            conv_part(step // 2, lax.rem(step, 2))
            block_part(step)

        @pl.when(step >= 2)
        def _():
            grid_part(step - 2)

    def store(part):
        return pltpu.make_async_copy(
            done.at[part],
            out.at[
                pl.ds((part // 2) * 8, 8), pl.ds(pl.multiple_of(lax.rem(part, 2) * 128, 128), 128)
            ],
            out_sem.at[part],
        )

    @pl.loop(0, 4)
    def _(part):
        others = back.at[part, pl.ds(0, 63)]
        pltpu.make_async_copy(others, others, back_recv_sem.at[part]).wait()
        y = back[part].reshape(1024, 256).astype(F32)
        y = mlp(y, gains[3:4, :], w_up.at[1], w_down.at[1])
        done[part] = y.astype(BF).reshape(8, 128, 256)
        store(part).start()

    @pl.loop(0, 4)
    def _(part):
        sent = send.at[part, pl.ds(0, 63)]
        pltpu.make_async_copy(sent, sent, go_send_sem.at[part]).wait()
        returned = ret.at[part, pl.ds(0, 63)]
        pltpu.make_async_copy(returned, returned, back_send_sem.at[part]).wait()
        store(part).wait()


def on_device(
    tokens,
    bn_scale,
    bn_shift,
    w_expand,
    b_expand,
    dw_kernel,
    dw_bias,
    w_project,
    b_project,
    norm_gains,
    attn_qkv,
    attn_out,
    rel_bias,
    mlp_up,
    mlp_down,
):
    vmem = pl.BlockSpec(memory_space=pltpu.VMEM)
    hbm = pl.BlockSpec(memory_space=pl.ANY)
    units = pltpu.VMEM((4, 64, 16, 256), BF)
    return pl.pallas_call(
        body,
        out_shape=jax.ShapeDtypeStruct((16, 256, 256), BF),
        in_specs=[hbm, vmem, vmem, hbm, vmem, vmem, vmem, hbm, vmem, vmem, hbm, hbm, vmem, hbm, hbm],
        out_specs=pl.BlockSpec(memory_space=pl.ANY),
        scratch_shapes=[
            pltpu.VMEM((16, 256, 256), BF),
            pltpu.VMEM((256, 1024), BF),
            pltpu.VMEM((1024, 256), BF),
            pltpu.VMEM((2, 256, 768), BF),
            pltpu.VMEM((2, 256, 256), BF),
            pltpu.VMEM((2, 256, 1024), BF),
            pltpu.VMEM((2, 1024, 256), BF),
            pltpu.VMEM((2, 18 * 256, 128), F32),
            pltpu.VMEM((18, 10, 32, 1024), BF),
            pltpu.VMEM((10, 16, 1024), BF),
            pltpu.VMEM((1024, 1024), BF),
            pltpu.VMEM((2, 1024, 128), F32),
            pltpu.VMEM((2, 16, 256), BF),
            pltpu.VMEM((2, 256, 256), BF),
            pltpu.VMEM((2, 3, 16, 256), BF),
            pltpu.VMEM((2, 48, 1024), F32),
            pltpu.VMEM((48, 256), F32),
            pltpu.VMEM((512, 128), F32),
            pltpu.VMEM((2, 64, 512), F32),
            units,
            units,
            pltpu.VMEM((2, 1024, 128), F32),
            pltpu.VMEM((2, 1024, 128), F32),
            units,
            units,
            pltpu.VMEM((4, 8, 128, 256), BF),
            pltpu.SemaphoreType.DMA((8,)),
            pltpu.SemaphoreType.DMA((8,)),
            pltpu.SemaphoreType.DMA((4,)),
            pltpu.SemaphoreType.DMA((4,)),
            pltpu.SemaphoreType.DMA((4,)),
            pltpu.SemaphoreType.DMA((4,)),
            pltpu.SemaphoreType.DMA((4,)),
            pltpu.SemaphoreType.DMA((7,)),
        ],
        compiler_params=pltpu.CompilerParams(
            collective_id=0, has_side_effects=True, vmem_limit_bytes=60 * 1024 * 1024
        ),
        cost_estimate=pl.CostEstimate(
            flops=20_000_000_000, bytes_accessed=8_000_000, transcendentals=20_000_000
        ),
        name="maxvit",
    )(
        tokens,
        bn_scale.reshape(1, -1),
        bn_shift.reshape(1, -1),
        w_expand,
        b_expand.reshape(1, -1),
        dw_kernel,
        dw_bias.reshape(1, -1),
        w_project,
        b_project.reshape(1, -1),
        norm_gains,
        attn_qkv,
        attn_out,
        rel_bias.reshape(16, 225),
        mlp_up,
        mlp_down,
    )


def solution(mesh):
    placed = (P("row", "col", None),) + (P(),) * 14
    return jax.shard_map(
        on_device, mesh=mesh, in_specs=placed, out_specs=P("row", "col", None), check_vma=False
    )
```
